128 devices in a mesh: ctx: 16 (over x_lo, z, core), dp: 8 (over y, x_hi).
Axes of the slice: x: 4 (x_hi: 2, x_lo: 2; x = x_hi * 2 + x_lo), y: 4, z: 4, core: 2. Of those that a mesh axis runs over, the one named last changes fastest.
Arguments:
- mixer_in: bfloat16 [32768, 10240], P(('dp', 'ctx')), parts along dimension 0, may hold values from -6 to 6
- step_raw: bfloat16 [32768, 128], P(('dp', 'ctx')), parts along dimension 0, may hold values from -3 to 176.032
- step_bias: float32 [128], replicated, may hold values from -4.6 to -2.3
- decay_log: float32 [128], replicated
- skip_gain: float32 [128], replicated, may hold values from 0.5 to 5
- conv_weight: float32 [4, 10240], replicated, may hold values from -3 to 3
- conv_bias: float32 [10240], replicated, may hold values from -3 to 3
- grad_out: bfloat16 [32768, 8192], P(('dp', 'ctx')), parts along dimension 0, may hold values from -6 to 6
Outputs:
- mixer_out: bfloat16 [32768, 8192], P(('dp', 'ctx')), parts along dimension 0
- grad_in: bfloat16 [32768, 10240], P(('dp', 'ctx')), parts along dimension 0
- grad_step: bfloat16 [32768, 128], P(('dp', 'ctx')), parts along dimension 0
- grad_conv_weight: float32 [32, 10240], P('dp'), parts along dimension 0
- grad_conv_bias: float32 [81920], P('dp'), parts along dimension 0
- grad_step_bias: float32 [1024], P('dp'), parts along dimension 0
- grad_decay_log: float32 [1024], P('dp'), parts along dimension 0
- grad_skip: float32 [1024], P('dp'), parts along dimension 0
The draws below stay inside these ranges and needn't reach their ends.
There are 8 independent parts, one for each index of `dp`. The reference program is written for one: setup_inputs(seed, part) draws one part's arguments, and reference() takes and returns one part's arrays. A program takes and returns all parts, laid end to end along the dimension named above; an argument that names none is the same for every part. Nothing has to cross between parts.
All inputs are finite; a program needn't handle non-finite values.
Results may differ from the reference program's by a relative error of at most 0.02.
Values may be sent and summed in bfloat16 or wider, within the bound.
A program may use at most 640 MiB of HBM per device.

```python
import math
import jax
import jax.numpy as jnp
from jax import lax

HEADS = 128
HEAD_DIM = 64
GROUPS = 8
STATE = 128
CONV = 4
BLOCK_ROWS = 256
SEQ = 4096
CHANNELS = 10240


def draw_step_raw(key, part):
    key = jax.random.fold_in(key, 11)
    first, second, third = jax.random.split(key, 3)
    base = jnp.clip(0.5 * jax.random.normal(first, (SEQ, HEADS), jnp.float32), -3.0, 3.0)
    spots = jax.random.randint(second, (4,), 0, SEQ)
    row_ids = jnp.arange(SEQ)[:, None]
    bursty = jnp.any(row_ids == spots[None, :], axis=1)
    height = 0.03 * SEQ * jax.random.uniform(third, (SEQ, HEADS), jnp.float32, 0.6, 1.4)
    return (base + jnp.where(bursty[:, None], height, 0.0)).astype(jnp.bfloat16)


def draw_decay_log(key, part):
    key = jax.random.fold_in(key, 23)
    slowest = -math.log(0.1 * SEQ)
    lower, upper = (slowest, math.log(0.5))
    return jax.random.uniform(key, (HEADS,), jnp.float32, lower, upper)


def levels(key, dims, cuts, least, largest):
    factor_of, own = 1.0, jax.random.fold_in(key, 6)
    for axis_at, blocks in cuts:
        steps = jnp.exp(jax.random.uniform(jax.random.fold_in(own, axis_at), (blocks,), jnp.float32, least / len(cuts), largest / len(cuts)))
        factor_of = factor_of * jnp.repeat(steps, dims[axis_at] // blocks).reshape([-1 if axis == axis_at else 1 for axis in range(len(dims))])
    return factor_of


def noise(own_key, shape, scale, most, cuts=(), kind=jnp.bfloat16):
    entries = scale * jax.random.normal(own_key, shape, jnp.float32)
    if cuts:
        entries = entries * levels(own_key, shape, cuts, -0.22, 0.18)
    return jnp.clip(entries, -most, most).astype(kind)


def setup_inputs(seed: int = 0, part: int = 0) -> dict:
    keys = jax.random.split(jax.random.key(seed), 9)
    own_keys = jax.random.split(jax.random.fold_in(keys[8], part), 9)
    mixer_in = noise(own_keys[0], (SEQ, CHANNELS), 1.0, 6.0, ((0, 16),))
    step_raw = draw_step_raw(jax.random.fold_in(jax.random.fold_in(keys[8], part), 71), part)
    step_bias = jnp.clip(jax.random.uniform(keys[2], (HEADS,), jnp.float32, -4.6, -2.3), -4.6, -2.3)
    decay_log = draw_decay_log(jax.random.fold_in(keys[8], 71), part)
    skip_gain = jnp.clip(jax.random.uniform(keys[4], (HEADS,), jnp.float32, 0.5, 5.0), 0.5, 5.0)
    conv_weight = noise(keys[5], (CONV, CHANNELS), CONV ** -0.5, 3.0, (), jnp.float32)
    conv_bias = noise(keys[6], (CHANNELS,), 0.5, 3.0, (), jnp.float32)
    grad_out = noise(own_keys[7], (SEQ, HEADS * HEAD_DIM), 1.0, 6.0, ((0, 16),))
    return {"mixer_in": mixer_in, "step_raw": step_raw, "step_bias": step_bias, "decay_log": decay_log, "skip_gain": skip_gain, "conv_weight": conv_weight, "conv_bias": conv_bias, "grad_out": grad_out}


def product(form, left, right):
    return jnp.einsum(form, left.astype(jnp.float32), right.astype(jnp.float32))

def block_scan(x_group, b_group, c_group, dt_group, rates, skip_group, start_state):
    length, heads, width = x_group.shape
    blocks = length // BLOCK_ROWS
    states_n = b_group.shape[1]
    x_blocks = x_group.reshape(blocks, BLOCK_ROWS, heads, width)
    b_blocks = b_group.reshape(blocks, BLOCK_ROWS, states_n)
    c_blocks = c_group.reshape(blocks, BLOCK_ROWS, states_n)
    step_sizes = dt_group.reshape(blocks, BLOCK_ROWS, heads)
    log_decay = jnp.cumsum(step_sizes * rates, axis=1)
    contact = product('ktn,kun->ktu', c_blocks, b_blocks)
    row_ids = lax.broadcasted_iota(jnp.int32, (BLOCK_ROWS, BLOCK_ROWS), 0)
    col_ids = lax.broadcasted_iota(jnp.int32, (BLOCK_ROWS, BLOCK_ROWS), 1)
    causal = (row_ids >= col_ids)[None, :, :, None]
    log_gaps = jnp.where(causal, log_decay[:, :, None, :] - log_decay[:, None, :, :], -1e+30)
    weights = jnp.exp(log_gaps) * step_sizes[:, None, :, :]
    scores = (contact[..., None] * weights).astype(jnp.bfloat16)
    within = product('ktuh,kuhp->kthp', scores, x_blocks)
    to_end = jnp.exp(log_decay[:, -1:, :] - log_decay) * step_sizes
    loaded = (b_blocks[:, :, :, None] * to_end[:, :, None, :]).astype(jnp.bfloat16)
    fresh_states = product('kunh,kuhp->khnp', loaded, x_blocks)
    block_fades = jnp.exp(log_decay[:, -1, :])

    def advance(running, pieces):
        fading, update = pieces
        return (fading[:, None, None] * running + update, running)
    last_state, entering = lax.scan(advance, start_state, (block_fades, fresh_states))
    carried = product('ktn,khnp->kthp', c_blocks, entering.astype(jnp.bfloat16)) * jnp.exp(log_decay)[..., None]
    result = within + carried + skip_group[None, None, :, None] * x_blocks.astype(jnp.float32)
    return (result.reshape(length, heads, width), last_state)

def mixer_core(x_act, b_act, c_act, dt_act, rates, skip_gain, start_state):
    length, heads, width = x_act.shape
    groups = b_act.shape[1]
    per_group = heads // groups
    states_n = b_act.shape[2]

    def single(pieces):
        return block_scan(*pieces)
    pieces = (jnp.moveaxis(x_act.reshape(length, groups, per_group, width), 1, 0), jnp.moveaxis(b_act, 1, 0), jnp.moveaxis(c_act, 1, 0), jnp.moveaxis(dt_act.reshape(length, groups, per_group), 1, 0), rates.reshape(groups, per_group), skip_gain.reshape(groups, per_group), start_state.reshape(groups, per_group, states_n, width))
    results, last_states = lax.map(single, pieces)
    return (jnp.moveaxis(results, 0, 1).reshape(length, heads, width), last_states.reshape(heads, states_n, width))

def conv_silu(padded, conv_weight, conv_bias):
    length = padded.shape[0] - conv_weight.shape[0] + 1
    summed = conv_bias + sum((conv_weight[k] * padded[k:k + length].astype(jnp.float32) for k in range(conv_weight.shape[0])))
    return jax.nn.silu(summed).astype(jnp.bfloat16)

def reference(mixer_in, step_raw, step_bias, decay_log, skip_gain, conv_weight, conv_bias, grad_out):
    inner_w = HEADS * HEAD_DIM
    group_cols = GROUPS * STATE

    def forward(mixer_in, step_raw, step_bias, decay_log, skip_gain, conv_weight, conv_bias):
        length = mixer_in.shape[0]
        padded = jnp.concatenate([jnp.zeros((CONV - 1, mixer_in.shape[1]), mixer_in.dtype), mixer_in], 0)
        activated = conv_silu(padded, conv_weight, conv_bias)
        x_act = activated[:, :inner_w].reshape(length, HEADS, HEAD_DIM)
        b_act = activated[:, inner_w:inner_w + group_cols].reshape(length, GROUPS, STATE)
        c_act = activated[:, inner_w + group_cols:].reshape(length, GROUPS, STATE)
        dt_act = jax.nn.softplus(step_raw.astype(jnp.float32) + step_bias)
        empty_state = jnp.zeros((HEADS, STATE, HEAD_DIM), jnp.float32)
        result, last_state = mixer_core(x_act, b_act, c_act, dt_act, -jnp.exp(decay_log), skip_gain, empty_state)
        return result.reshape(length, inner_w)
    result, pullback = jax.vjp(forward, mixer_in, step_raw, step_bias, decay_log, skip_gain, conv_weight, conv_bias)
    cotangents = pullback(grad_out.astype(jnp.float32))
    return (result.astype(jnp.bfloat16), cotangents[0], cotangents[1], cotangents[5], cotangents[6], cotangents[2], cotangents[3], cotangents[4])
```

```python
import functools
import math

import jax
import jax.numpy as jnp
from jax import lax
from jax.experimental import pallas as pl
from jax.experimental.pallas import tpu as pltpu
from jax.sharding import PartitionSpec as P

HEADS = 128
HEAD_DIM = 64
GROUPS = 8
STATE = 128
CONV = 4
ROWS = 256
INNER = HEADS * HEAD_DIM
SPAN = GROUPS * STATE
WIDTH = INNER // GROUPS
PAIRS = WIDTH // 128
CHUNKS = 16
LOG2E = math.log2(math.e)
F32 = jnp.float32
BF16 = jnp.bfloat16
MESH = pl.DeviceIdType.MESH
VMEM_LIMIT = 56 * 1024 * 1024


def dot(left, right):
    return jnp.dot(left, right, preferred_element_type=F32)


def dot_nt(left, right):
    return lax.dot_general(left, right, (((1,), (1,)), ((), ())), preferred_element_type=F32)


def dot_tn(left, right):
    return lax.dot_general(left, right, (((0,), (0,)), ((), ())), preferred_element_type=F32)


def low_half():
    return lax.broadcasted_iota(jnp.int32, (ROWS, 128), 1) < HEAD_DIM


def pair_columns(values, first):
    turned = pltpu.roll(values, lax.rem(128 - first, 128), 1)
    return (
        jnp.broadcast_to(turned[:, 0:1], (ROWS, 128)),
        jnp.broadcast_to(turned[:, 1:2], (ROWS, 128)),
    )


def taps_of(raw, halo):
    both = jnp.concatenate([halo[8:16].astype(F32), raw.astype(F32)], 0)
    return [
        (both if k == CONV - 1 else pltpu.roll(both, CONV - 1 - k, 0))[8:] for k in range(CONV)
    ]


def conv_act(raw, halo, weight, bias):
    taps = taps_of(raw, halo)
    pre = bias + sum(weight[k : k + 1] * taps[k] for k in range(CONV))
    gate = 1.0 / (1.0 + jnp.exp(-pre))
    act = pre * gate
    return act, gate + act * (1.0 - gate)


def conv_back(dpre, raw, halo, weight):
    both = jnp.concatenate([dpre, jnp.zeros((8, dpre.shape[1]), F32)], 0)
    grad = weight[CONV - 1 : CONV] * dpre
    for k in range(CONV - 1):
        shift = CONV - 1 - k
        grad = grad + weight[k : k + 1] * pltpu.roll(both, ROWS + 8 - shift, 0)[:ROWS]
    taps = taps_of(raw, halo)
    sums = [jnp.sum(dpre * tap, 0, keepdims=True) for tap in taps]
    sums.append(jnp.sum(dpre, 0, keepdims=True))
    sums.append(jnp.zeros((3, dpre.shape[1]), F32))
    return grad, jnp.concatenate(sums, 0)


def steps_kernel(raw_ref, bias_ref, decay_ref, dt_ref, ld_ref, ldt_ref):
    dt = jax.nn.softplus(raw_ref[...].astype(F32) + bias_ref[...])
    ld = dt * (-jnp.exp(decay_ref[...]) * LOG2E)
    rows = lax.broadcasted_iota(jnp.int32, (ROWS, HEADS), 0)
    shift = 1
    while shift < ROWS:
        ld = ld + jnp.where(rows >= shift, pltpu.roll(ld, shift, 0), 0.0)
        shift *= 2
    dt_ref[...] = dt
    ld_ref[...] = ld
    ldt_ref[...] = ld.T


def state_kernel(
    x_ref, b_ref, c_ref, hx_ref, hb_ref, hc_ref, wx_ref, wb_ref, wc_ref, vx_ref, vb_ref, vc_ref,
    dy_ref, dt_ref, ld_ref,
    xa_ref, ba_ref, ca_ref, sx_ref, sb_ref, sc_ref, fg_ref, fade_ref,
    bt, ct,
):
    group = pl.program_id(0)
    for raw, halo, weight, bias, act_o, slope_o, turned in (
        (b_ref, hb_ref, wb_ref, vb_ref, ba_ref, sb_ref, bt),
        (c_ref, hc_ref, wc_ref, vc_ref, ca_ref, sc_ref, ct),
    ):
        act, slope = conv_act(raw[...], halo[...], weight[...], bias[...])
        act_o[...] = act.astype(BF16)
        slope_o[...] = slope.astype(BF16)
        turned[...] = act.T.astype(BF16)
    low = low_half()

    def body(j, carry):
        lanes = pl.ds(pl.multiple_of(j * 128, 128), 128)
        act, slope = conv_act(x_ref[:, lanes], hx_ref[:, lanes], wx_ref[:, lanes], vx_ref[:, lanes])
        act = act.astype(BF16)
        xa_ref[:, lanes] = act
        sx_ref[:, lanes] = slope.astype(BF16)
        first = group * (2 * PAIRS) + 2 * j
        ld = jnp.where(low, *pair_columns(ld_ref[...], first))
        dt = jnp.where(low, *pair_columns(dt_ref[...], first))
        last = ld[ROWS - 1 : ROWS]
        scaled = (act.astype(F32) * dt).astype(BF16)
        ends = (scaled.astype(F32) * jnp.exp2(last - ld)).astype(BF16)
        begins = (dy_ref[:, lanes].astype(F32) * jnp.exp2(ld)).astype(BF16)
        fg_ref[0, 0, :, lanes] = dot(bt[...], ends).astype(BF16)
        fg_ref[1, 0, :, lanes] = dot(ct[...], begins).astype(BF16)
        fade_ref[0, :, lanes] = jnp.exp2(last)
        return carry

    lax.fori_loop(0, PAIRS, body, 0)


def chain_kernel(fg, fade, ed, given, above, below, fades, sems, fade_sems):
    index = lax.axis_index("ctx")
    count = lax.axis_size("ctx")
    core, chip = lax.rem(index, 2), index // 2
    own = 1 - core
    partner = index + 1 - 2 * core
    ahead = lax.rem(index + 2, count)
    behind = lax.rem(index + count - 2, count)
    down = jnp.where(core == 1, ahead, behind)
    place = jnp.where(core == 1, chip, count // 2 - 1 - chip)
    has_up = place > 0
    has_down = place < count // 2 - 1

    barrier = pltpu.get_barrier_semaphore()
    for other in (partner, ahead, behind):
        pl.semaphore_signal(barrier, inc=1, device_id={"ctx": other}, device_id_type=MESH)
    pl.semaphore_wait(barrier, 3)

    def copy(kind, q, src, dst, to):
        return pltpu.make_async_remote_copy(
            src_ref=src, dst_ref=dst, send_sem=sems.at[0, kind, q], recv_sem=sems.at[1, kind, q],
            device_id={"ctx": to}, device_id_type=MESH,
        )

    fade_copy = pltpu.make_async_remote_copy(
        src_ref=fade, dst_ref=fades, send_sem=fade_sems.at[0], recv_sem=fade_sems.at[1],
        device_id={"ctx": partner}, device_id_type=MESH,
    )
    fade_copy.start()

    def give(q):
        return copy(0, q, fg.at[core, q], given.at[q], partner)

    def pass_on(q):
        return copy(1, q, below.at[q], above.at[q], down)

    def share(q):
        return copy(2, q, above.at[q], ed.at[own, q], partner)

    def start_give(q, carry):
        give(q).start()
        return carry

    lax.fori_loop(0, CHUNKS, start_give, 0)

    @pl.when(jnp.logical_not(has_up))
    def _():
        above[...] = jnp.zeros_like(above)

    fade_copy.wait()

    def step(q, carry):
        group = q // (CHUNKS // GROUPS)
        mine = fade[pl.ds(group, 1), :]
        theirs = fades[pl.ds(group, 1), :]
        give(q).wait_recv()
        got = given[q].astype(F32)

        @pl.when(has_up)
        def _():
            pass_on(q).wait_recv()

        arrived = above[q].astype(F32)

        @pl.when(has_down)
        def _():
            total = fg[own, q].astype(F32) + mine * (got + theirs * arrived)
            below[q] = total.astype(BF16)
            pass_on(q).start()

        share(q).start()
        ed[own, q] = (got + theirs * arrived).astype(BF16)
        return carry

    lax.fori_loop(0, CHUNKS, step, 0)

    def finish(q, carry):
        give(q).wait_send()

        @pl.when(has_down)
        def _():
            pass_on(q).wait_send()

        share(q).wait()
        return carry

    lax.fori_loop(0, CHUNKS, finish, 0)


def main_kernel(
    x_ref, b_ref, c_ref, hx_ref, hb_ref, hc_ref, wx_ref, wb_ref, wc_ref,
    xa_ref, ba_ref, ca_ref, sx_ref, sb_ref, sc_ref, dy_ref, dt_ref, ld_ref, ldt_ref,
    ed_ref, fade_ref, skip_ref,
    y_ref, gx_ref, gb_ref, gc_ref, dx8_ref, db8_ref, dc8_ref, wgx_ref, wgb_ref, wgc_ref,
    rk_ref, kk_ref, sums_ref,
    contact, dcontact, db, dc,
):
    group = pl.program_id(0)
    b = ba_ref[...]
    c = ca_ref[...]
    contact[...] = dot_nt(c, b)
    dcontact[...] = jnp.zeros_like(dcontact)
    db[...] = jnp.zeros_like(db)
    dc[...] = jnp.zeros_like(dc)
    low = low_half()
    lane = lax.broadcasted_iota(jnp.int32, (ROWS, 128), 1)
    causal = lax.broadcasted_iota(jnp.int32, (ROWS, ROWS), 0) >= lax.broadcasted_iota(
        jnp.int32, (ROWS, ROWS), 1
    )
    rk_ref[0] = jnp.zeros((ROWS, 128), F32)
    kk_ref[0] = jnp.zeros((ROWS, 128), F32)

    def body(j, carry):
        lanes = pl.ds(pl.multiple_of(j * 128, 128), 128)
        first = group * (2 * PAIRS) + 2 * j
        lds = pair_columns(ld_ref[...], first)
        ld = jnp.where(low, *lds)
        dt = jnp.where(low, *pair_columns(dt_ref[...], first))
        act = xa_ref[:, lanes].astype(F32)
        dy = dy_ref[:, lanes]
        dyf = dy.astype(F32)
        scaled = (act * dt).astype(BF16)
        scaledf = scaled.astype(F32)
        state = ed_ref[0, 0, :, lanes]
        dstate = ed_ref[1, 0, :, lanes]
        to_end = jnp.exp2(ld[ROWS - 1 : ROWS] - ld)
        from_start = jnp.exp2(ld)
        ends = (scaledf * to_end).astype(BF16)
        begins = (dyf * from_start).astype(BF16)
        db[...] += dot_nt(ends, dstate)
        dc[...] += dot_nt(begins, state)
        inner = dot(c, state) * from_start
        dload = dot(b, dstate) * to_end
        dscaled = dload
        zero = jnp.zeros_like(dy)
        for half in range(2):
            side = low if half == 0 else jnp.logical_not(low)
            wide = jnp.concatenate([lds[half], lds[half]], 1)
            gap = wide - ldt_ref[pl.ds(first + half, 1), :]
            decay = jnp.exp2(jnp.where(causal, gap, -1e30))
            dy_half = jnp.where(side, dy, zero)
            scaled_half = jnp.where(side, scaled, zero)
            scores = (contact[...] * decay).astype(BF16)
            dcontact[...] += dot_nt(dy_half, scaled) * decay
            inner = inner + dot(scores, scaled_half)
            dscaled = dscaled + dot_tn(scores, dy_half)
        skip = skip_ref[:, lanes]
        y_ref[:, lanes] = (inner + skip * act).astype(BF16)
        grow = scaledf * dscaled
        net = dyf * inner - grow
        for half in range(2):
            side = low if half == 0 else jnp.logical_not(low)
            here = lane == 2 * j + half
            rk_ref[0] = jnp.where(
                here, jnp.sum(jnp.where(side, net, 0.0), 1, keepdims=True), rk_ref[0]
            )
            kk_ref[0] = jnp.where(
                here, jnp.sum(jnp.where(side, grow, 0.0), 1, keepdims=True), kk_ref[0]
            )
        ends_sum = jnp.sum(scaledf * dload, 0, keepdims=True)
        fade = fade_ref[0, :, lanes]
        ends_sum = ends_sum + fade * jnp.sum(
            state.astype(F32) * dstate.astype(F32), 0, keepdims=True
        )
        skip_sum = jnp.sum(dyf * act, 0, keepdims=True)
        sums_ref[:, lanes] = jnp.concatenate([ends_sum, skip_sum, jnp.zeros((6, 128), F32)], 0)
        dpre = (dt * dscaled + skip * dyf) * sx_ref[:, lanes].astype(F32)
        dx8_ref[:, lanes] = dpre[:8]
        grad, wsum = conv_back(dpre, x_ref[:, lanes], hx_ref[:, lanes], wx_ref[:, lanes])
        gx_ref[:, lanes] = grad.astype(BF16)
        wgx_ref[:, lanes] = wsum
        return carry

    lax.fori_loop(0, PAIRS, body, 0)
    dcon = dcontact[...].astype(BF16)
    for total, slope, raw, halo, weight, first8, grad_o, sum_o in (
        (db[...] + dot_tn(dcon, c), sb_ref, b_ref, hb_ref, wb_ref, db8_ref, gb_ref, wgb_ref),
        (dc[...] + dot(dcon, b), sc_ref, c_ref, hc_ref, wc_ref, dc8_ref, gc_ref, wgc_ref),
    ):
        dpre = total * slope[...].astype(F32)
        first8[...] = dpre[:8]
        grad, wsum = conv_back(dpre, raw[...], halo[...], weight[...])
        grad_o[...] = grad.astype(BF16)
        sum_o[...] = wsum


def params(**kw):
    return pltpu.CompilerParams(vmem_limit_bytes=VMEM_LIMIT, **kw)


def on_device(
    mixer_in, step_raw, step_bias, decay_log, skip_gain, conv_weight, conv_bias, grad_out
):
    count = lax.axis_size("ctx")
    halo = lax.ppermute(mixer_in[ROWS - 16 :], "ctx", [(i, i + 1) for i in range(count - 1)])
    bias_row = conv_bias[None]
    skip_row = jnp.repeat(skip_gain, HEAD_DIM)[None]
    sds = jax.ShapeDtypeStruct
    dt, ld, ldt = pl.pallas_call(
        steps_kernel,
        out_shape=[sds((ROWS, HEADS), F32), sds((ROWS, HEADS), F32), sds((HEADS, ROWS), F32)],
        compiler_params=params(),
        name="steps",
    )(step_raw, step_bias[None], decay_log[None])

    def cols(rows, kind):
        if kind == "x":
            return pl.BlockSpec((rows, WIDTH), lambda g: (0, g))
        base = (INNER + (SPAN if kind == "c" else 0)) // STATE
        return pl.BlockSpec((rows, STATE), lambda g: (0, base + g))

    def own_cols(rows, wide):
        return pl.BlockSpec((rows, WIDTH if wide else STATE), lambda g: (0, g))

    def whole(shape):
        return pl.BlockSpec(shape, lambda g: (0,) * len(shape))

    state_spec = pl.BlockSpec((2, 1, STATE, WIDTH), lambda g: (0, g, 0, 0))
    fade_spec = pl.BlockSpec((1, 1, WIDTH), lambda g: (g, 0, 0))
    three = ("x", "b", "c")
    xa, ba, ca, sx, sb, sc, fg, fade = pl.pallas_call(
        state_kernel,
        grid=(GROUPS,),
        in_specs=[cols(ROWS, k) for k in three]
        + [cols(16, k) for k in three]
        + [cols(CONV, k) for k in three]
        + [cols(1, k) for k in three]
        + [own_cols(ROWS, True), whole((ROWS, HEADS)), whole((ROWS, HEADS))],
        out_specs=[own_cols(ROWS, True), own_cols(ROWS, False), own_cols(ROWS, False)] * 2
        + [state_spec, fade_spec],
        out_shape=[sds((ROWS, INNER), BF16), sds((ROWS, SPAN), BF16), sds((ROWS, SPAN), BF16)] * 2
        + [sds((2, GROUPS, STATE, WIDTH), BF16), sds((GROUPS, 1, WIDTH), F32)],
        scratch_shapes=[pltpu.VMEM((STATE, ROWS), BF16)] * 2,
        compiler_params=params(),
        name="block_states",
    )(
        *[mixer_in] * 3, *[halo] * 3, *[conv_weight] * 3, *[bias_row] * 3, grad_out, dt, ld
    )

    piece = STATE * GROUPS // CHUNKS
    vmem = pl.BlockSpec(memory_space=pltpu.VMEM)
    ed = pl.pallas_call(
        chain_kernel,
        in_specs=[vmem, vmem],
        out_specs=vmem,
        out_shape=sds((2, CHUNKS, piece, WIDTH), BF16),
        scratch_shapes=[pltpu.VMEM((CHUNKS, piece, WIDTH), BF16)] * 3
        + [
            pltpu.VMEM((GROUPS, WIDTH), F32),
            pltpu.SemaphoreType.DMA((2, 3, CHUNKS)),
            pltpu.SemaphoreType.DMA((2,)),
        ],
        compiler_params=params(collective_id=1, has_side_effects=True),
        name="chain",
    )(fg.reshape(2, CHUNKS, piece, WIDTH), fade.reshape(GROUPS, WIDTH))
    ed = ed.reshape(2, GROUPS, STATE, WIDTH)

    slab = pl.BlockSpec((1, ROWS, 128), lambda g: (g, 0, 0))
    outs = pl.pallas_call(
        main_kernel,
        grid=(GROUPS,),
        in_specs=[cols(ROWS, k) for k in three]
        + [cols(16, k) for k in three]
        + [cols(CONV, k) for k in three]
        + [own_cols(ROWS, True), own_cols(ROWS, False), own_cols(ROWS, False)] * 2
        + [own_cols(ROWS, True), whole((ROWS, HEADS)), whole((ROWS, HEADS)), whole((HEADS, ROWS))]
        + [state_spec, fade_spec, own_cols(1, True)],
        out_specs=[own_cols(ROWS, True)]
        + [own_cols(ROWS, True), own_cols(ROWS, False), own_cols(ROWS, False)]
        + [own_cols(8, True), own_cols(8, False), own_cols(8, False)] * 2
        + [slab, slab, own_cols(8, True)],
        out_shape=[sds((ROWS, INNER), BF16)]
        + [sds((ROWS, INNER), BF16), sds((ROWS, SPAN), BF16), sds((ROWS, SPAN), BF16)]
        + [sds((8, INNER), F32), sds((8, SPAN), F32), sds((8, SPAN), F32)] * 2
        + [sds((GROUPS, ROWS, 128), F32)] * 2
        + [sds((8, INNER), F32)],
        scratch_shapes=[pltpu.VMEM((ROWS, ROWS), F32)] * 2 + [pltpu.VMEM((ROWS, STATE), F32)] * 2,
        compiler_params=params(),
        name="mixer",
    )(
        *[mixer_in] * 3, *[halo] * 3, *[conv_weight] * 3, xa, ba, ca, sx, sb, sc, grad_out,
        dt, ld, ldt, ed, fade, skip_row,
    )
    mixer_out, gx, gb, gc, dx8, db8, dc8, wgx, wgb, wgc, rk, kk, sums = outs

    first = jnp.concatenate([dx8, db8, dc8], 1)[: CONV - 1].astype(BF16)
    after = lax.ppermute(first, "ctx", [(i + 1, i) for i in range(count - 1)]).astype(F32)
    more = jnp.stack(
        [
            sum(conv_weight[k] * after[s - k] for k in range(s + 1))
            for s in range(CONV - 1)
        ]
    )
    grad_in = jnp.concatenate([gx, gb, gc], 1)
    tail = grad_in[ROWS - CONV + 1 :].astype(F32) + more
    grad_in = lax.dynamic_update_slice(grad_in, tail.astype(BF16), (ROWS - CONV + 1, 0))

    def heads_of(slabs):
        return jnp.moveaxis(slabs[:, :, : 2 * PAIRS], 0, 1).reshape(ROWS, HEADS)

    net, grow = heads_of(rk), heads_of(kk)
    ends = sums[0].reshape(HEADS, HEAD_DIM).sum(1)
    skips = sums[1].reshape(HEADS, HEAD_DIM).sum(1)
    later = (jnp.arange(ROWS)[:, None] <= jnp.arange(ROWS)[None, :]).astype(F32)
    dlog = jnp.dot(later, net, precision=lax.Precision.HIGHEST) + ends
    rates = -jnp.exp(decay_log)
    ddt = grow / dt + rates * dlog
    gate = jax.nn.sigmoid(step_raw.astype(F32) + step_bias)
    dstep = ddt * gate
    packed = jnp.concatenate(
        [
            jnp.concatenate([wgx, wgb, wgc], 1)[: CONV + 1].reshape(-1),
            dstep.sum(0),
            rates * (dlog * dt).sum(0),
            skips,
        ]
    )
    packed = lax.psum(packed.astype(BF16), "ctx").astype(F32)
    channels = INNER + 2 * SPAN
    gw = packed[: CONV * channels].reshape(CONV, channels)
    gv = packed[CONV * channels : (CONV + 1) * channels]
    rest = packed[(CONV + 1) * channels :].reshape(3, HEADS)
    return (mixer_out, grad_in, dstep.astype(BF16), gw, gv, rest[0], rest[1], rest[2])


def solution(mesh):
    rows = P(("dp", "ctx"), None)
    in_specs = (rows, rows, P(), P(), P(), P(), P(), rows)
    out_specs = (rows, rows, rows, P("dp", None), P("dp"), P("dp"), P("dp"), P("dp"))
    return jax.shard_map(
        on_device, mesh=mesh, in_specs=in_specs, out_specs=out_specs, check_vma=False
    )
```

```python
import functools
import math

import jax
import jax.numpy as jnp
from jax import lax
from jax.experimental import pallas as pl
from jax.experimental.pallas import tpu as pltpu
from jax.sharding import PartitionSpec as P

HEADS = 128
HEAD_DIM = 64
GROUPS = 8
STATE = 128
CONV = 4
ROWS = 256
HALF = ROWS // 2
INNER = HEADS * HEAD_DIM
SPAN = GROUPS * STATE
CHANNELS = INNER + 2 * SPAN
WIDTH = INNER // GROUPS
PAIRS = WIDTH // 128
BLOCKS = CHANNELS // WIDTH
CHUNKS = 16
PIECE = STATE * GROUPS // CHUNKS
BEAT = 4
LAG = 3
LEAD = 3
LOG2E = math.log2(math.e)
F32 = jnp.float32
BF16 = jnp.bfloat16
MESH = pl.DeviceIdType.MESH
VMEM_LIMIT = 56 * 1024 * 1024


def dot(left, right):
    return jnp.dot(left, right, preferred_element_type=F32)


def dot_nt(left, right):
    return lax.dot_general(left, right, (((1,), (1,)), ((), ())), preferred_element_type=F32)


def dot_tn(left, right):
    return lax.dot_general(left, right, (((0,), (0,)), ((), ())), preferred_element_type=F32)


def pair_columns(values, first):
    return tuple(
        jnp.broadcast_to(values[:, first + i : first + i + 1], (ROWS, 128)) for i in range(2)
    )


def pair_lanes(values, first, low):
    return jnp.where(low, *pair_columns(values, first))


def head_picks():
    lanes = lax.broadcasted_iota(jnp.int32, (WIDTH, HEADS), 0)
    heads = lax.broadcasted_iota(jnp.int32, (WIDTH, HEADS), 1)
    return (heads == lanes // HEAD_DIM).astype(F32).astype(BF16)


def low_half():
    return lax.broadcasted_iota(jnp.int32, (ROWS, 128), 1) < HEAD_DIM


def lanes_at(j):
    if isinstance(j, int):
        return slice(j * 128, (j + 1) * 128)
    return pl.ds(pl.multiple_of(j * 128, 128), 128)


def stack(*pieces):
    return jnp.concatenate(pieces, 0)


def beside(*pieces):
    return jnp.concatenate(pieces, 1)


def scores_of(group, j, dy_ref, scaled_ref, ldg_ref, ldt_ref, contact, dcontact, in_ref, ds_ref):
    lanes = lanes_at(j)
    first = group * (2 * PAIRS) + 2 * j
    low = low_half()
    rows = lax.broadcasted_iota(jnp.int32, (HALF, HALF), 0)
    causal = rows >= lax.broadcasted_iota(jnp.int32, (HALF, HALF), 1)
    dy = dy_ref[:, lanes]
    scaled = scaled_ref[:, lanes]
    zero = jnp.zeros_like(dy)
    dys = (jnp.where(low, dy, zero), jnp.where(low, zero, dy))
    xs = (jnp.where(low, scaled, zero), jnp.where(low, zero, scaled))
    top = dot_nt(stack(dys[0][:HALF], dys[1][:HALF]), scaled[:HALF])
    bottom = dot_nt(stack(dys[0][HALF:], dys[1][HALF:]), scaled)
    lds = pair_columns(ldg_ref[...], 2 * j)
    tiles = []
    for half in range(2):
        row = ldt_ref[pl.ds(first + half, 1), :]
        here = slice(HALF * half, HALF * half + HALF)
        for tile, mine, cols, grad in (
            (0, slice(0, HALF), slice(0, HALF), top[here]),
            (1, slice(HALF, ROWS), slice(0, HALF), bottom[here, :HALF]),
            (2, slice(HALF, ROWS), slice(HALF, ROWS), bottom[here, HALF:]),
        ):
            gap = lds[half][mine] - row[:, cols]
            if tile != 1:
                gap = jnp.where(causal, gap, -1e30)
            decay = jnp.exp2(gap)
            tiles.append((contact[tile] * decay).astype(BF16))
            dcontact[tile] += grad * decay
    in_ref[:HALF, lanes] = dot(beside(tiles[0], tiles[3]), stack(xs[0][:HALF], xs[1][:HALF]))
    in_ref[HALF:, lanes] = dot(beside(tiles[1], tiles[2], tiles[4], tiles[5]), stack(*xs))
    ds_ref[:HALF, lanes] = dot_tn(stack(tiles[0], tiles[1], tiles[3], tiles[4]), stack(*dys))
    ds_ref[HALF:, lanes] = dot_tn(stack(tiles[2], tiles[5]), stack(dys[0][HALF:], dys[1][HALF:]))


def start_tiles(b, c, contact, dcontact):
    contact[0] = dot_nt(c[:HALF], b[:HALF])
    both = dot_nt(c[HALF:], b)
    contact[1] = both[:, :HALF]
    contact[2] = both[:, HALF:]
    dcontact[...] = jnp.zeros_like(dcontact)


def end_tiles(b, c, dcontact, dbw_ref, dcw_ref):
    tiles = dcontact[...].astype(BF16)
    dbw_ref[:HALF] = dot_tn(stack(tiles[0], tiles[1]), c)
    dbw_ref[HALF:] = dot_tn(tiles[2], c[HALF:])
    dcw_ref[:HALF] = dot(tiles[0], b[:HALF])
    dcw_ref[HALF:] = dot(beside(tiles[1], tiles[2]), b)


def block_kernel(
    raw_ref, mixer_ref, weight_ref, bias_ref, dy_ref, step_ref, step_bias_ref, decay_ref, skip_ref,
    act_ref, slope_ref, scaled_ref, in_ref, ds_ref, dbw_ref, dcw_ref,
    ed, halo_ref, fade_ref, skips, dt_ref, dtg, ldg,
    halo, fade, came, ldt, turned, shifted, bc, xs, fg, given, above, below, fades, contact, dcontact,
    sems, edge_sems,
):
    at = pl.program_id(0)
    index = lax.axis_index("ctx")
    count = lax.axis_size("ctx")
    core, chip = lax.rem(index, 2), index // 2
    own = 1 - core
    partner = index + 1 - 2 * core
    ahead = lax.rem(index + 2, count)
    behind = lax.rem(index + count - 2, count)
    down = jnp.where(core == 1, ahead, behind)
    place = jnp.where(core == 1, chip, count // 2 - 1 - chip)
    has_up = place > 0
    has_down = place < count // 2 - 1
    after = lax.rem(index + 1, count)
    before = lax.rem(index + count - 1, count)

    def remote(src, dst, send, recv, to):
        return pltpu.make_async_remote_copy(
            src_ref=src, dst_ref=dst, send_sem=send, recv_sem=recv,
            device_id={"ctx": to}, device_id_type=MESH,
        )

    def copy(kind, q, src, dst, to):
        return remote(src, dst, sems.at[0, kind, q], sems.at[1, kind, q], to)

    def give(q):
        return copy(0, q, fg.at[core, q], given.at[q], partner)

    def pass_on(q):
        return copy(1, q, below.at[q], above.at[q], down)

    def share(q):
        return copy(2, q, above.at[q], came.at[q], partner)

    tail = mixer_ref.at[pl.ds(ROWS - 16, 16), :]
    edge_copy = remote(tail, halo, edge_sems.at[0], edge_sems.at[1], after)
    fade_copy = remote(fade, fades, edge_sems.at[2], edge_sems.at[3], partner)

    @pl.when(at == 0)
    def _():
        barrier = pltpu.get_barrier_semaphore()
        for other in (partner, ahead, behind, after, before):
            pl.semaphore_signal(barrier, inc=1, device_id={"ctx": other}, device_id_type=MESH)
        pl.semaphore_wait(barrier, 5)
        edge_copy.start()

        dt = jax.nn.softplus(step_ref[...].astype(F32) + step_bias_ref[...])
        ld = dt * (-jnp.exp(decay_ref[...]) * LOG2E)
        rows = lax.broadcasted_iota(jnp.int32, (ROWS, HEADS), 0)
        shift = 1
        while shift < ROWS:
            ld = ld + jnp.where(rows >= shift, pltpu.roll(ld, shift, 0), 0.0)
            shift *= 2
        dt_ref[...] = dt
        ldt[...] = ld.T
        for group in range(GROUPS):
            shift = (HEADS - group * 2 * PAIRS) % HEADS
            dtg[group] = pltpu.roll(dt, shift, 1) if shift else dt
            ldg[group] = pltpu.roll(ld, shift, 1) if shift else ld
        low = lax.broadcasted_iota(jnp.int32, (1, 128), 1) < HEAD_DIM
        for row, out in ((jnp.exp2(ld[ROWS - 1 : ROWS]), fade), (skip_ref[...], skips)):
            for group in range(GROUPS):
                for j in range(PAIRS):
                    at_head = group * 2 * PAIRS + 2 * j
                    pair = [
                        jnp.broadcast_to(row[:, at_head + i : at_head + i + 1], (1, 128))
                        for i in range(2)
                    ]
                    out[group : group + 1, lanes_at(j)] = jnp.where(low, *pair)
        fade_copy.start()

        @pl.when(jnp.logical_not(has_up))
        def _():
            above[...] = jnp.zeros_like(above)

        edge_copy.wait()

        @pl.when(index == 0)
        def _():
            halo[...] = jnp.zeros_like(halo)

        halo_ref[...] = halo[...]
        fade_ref[...] = fade[...]
        fade_copy.wait()

    def serve(q):
        block = q // (CHUNKS // GROUPS)
        mine = fade[pl.ds(block, 1), :]
        theirs = fades[pl.ds(block, 1), :]
        give(q).wait_recv()
        got = given[q].astype(F32)

        @pl.when(has_up)
        def _():
            pass_on(q).wait_recv()

        here = got + theirs * above[q].astype(F32)

        @pl.when(has_down)
        def _():
            below[q] = (fg[own, q].astype(F32) + mine * here).astype(BF16)
            pass_on(q).start()

        share(q).start()
        ed[own, q] = here.astype(BF16)

    def serve_at(slot):
        q = slot - LEAD - LAG * place
        pl.when(jnp.logical_and(q >= 0, q < CHUNKS))(functools.partial(serve, q))

    def conv(j):
        lanes = lanes_at(j)
        slot = j % 2
        here = pl.ds(pl.multiple_of(lax.rem(at + GROUPS, BLOCKS) * WIDTH + j * 128, 128), 128)
        shifted[slot, 0:8, :] = halo[8:16, here].astype(F32)
        raw = raw_ref[:, lanes].astype(F32)
        shifted[slot, 8 : ROWS + 8, :] = raw
        pre = bias_ref[:, lanes] + weight_ref[CONV - 1 : CONV, lanes] * raw
        for k in range(CONV - 1):
            pre = pre + weight_ref[k : k + 1, lanes] * shifted[slot, 5 + k : ROWS + 5 + k, :]
        gate = 1.0 / (1.0 + jnp.exp(-pre))
        act = pre * gate
        slope_ref[:, lanes] = (gate + act * (1.0 - gate)).astype(BF16)
        rounded = act.astype(BF16)
        act_ref[:, lanes] = rounded
        return rounded

    @pl.when(at < 2)
    def _():
        for j in range(PAIRS):
            act = conv(j)
            bc[at, :, lanes_at(j)] = act
            turned[at, j * STATE : (j + 1) * STATE, :] = act.T

    @pl.when(jnp.logical_and(at >= 2, at < BLOCKS))
    def _():
        group = at - 2
        mine = pl.ds(pl.multiple_of(group * STATE, STATE), STATE)
        per = CHUNKS // GROUPS
        low = low_half()
        for j in range(PAIRS):
            if j % BEAT == 0:
                serve_at((group * PAIRS + j) // BEAT)
            lanes = lanes_at(j)
            act = conv(j)
            ld = pair_lanes(ldg[group], 2 * j, low)
            dt = pair_lanes(dtg[group], 2 * j, low)
            last = ld[ROWS - 1 : ROWS]
            scaled = (act.astype(F32) * dt).astype(BF16)
            scaled_ref[:, lanes] = scaled
            xs[group, :, lanes] = scaled
            ends = (scaled.astype(F32) * jnp.exp2(last - ld)).astype(BF16)
            begins = (dy_ref[:, lanes].astype(F32) * jnp.exp2(ld)).astype(BF16)
            for kind, piece in ((0, ends), (1, begins)):
                state = dot(turned[kind, mine, :], piece).astype(BF16)
                fg[kind, pl.ds(group * per, per), :, lanes] = state.reshape(per, PIECE, 128)

        def start_give(r, carry):
            give(group * per + r).start()
            return carry

        lax.fori_loop(0, per, start_give, 0)

    @pl.when(at >= BLOCKS)
    def _():
        group = at - BLOCKS
        here = lanes_at(group)
        b = bc[0, :, here]
        c = bc[1, :, here]
        start_tiles(b, c, contact, dcontact)
        for j in range(PAIRS):
            if j % BEAT == 0:
                serve_at((GROUPS * PAIRS + group * PAIRS + j) // BEAT)
            scores_of(
                group, j, dy_ref, xs.at[group], ldg.at[group], ldt, contact, dcontact, in_ref, ds_ref
            )
        end_tiles(b, c, dcontact, dbw_ref, dcw_ref)

    @pl.when(at == BLOCKS + GROUPS - 1)
    def _():
        def late(slot, carry):
            serve_at(slot)
            return carry

        done = 2 * GROUPS * PAIRS // BEAT
        lax.fori_loop(done, max(done, LEAD + 7 * LAG + CHUNKS), late, 0)

        def finish(q, carry):
            give(q).wait_send()

            @pl.when(has_down)
            def _():
                pass_on(q).wait_send()

            share(q).wait()
            ed[core, q] = came[q]
            return carry

        lax.fori_loop(0, CHUNKS, finish, 0)


def finish_kernel(
    raw_ref, halo_ref, weight_ref, slope_ref, act_ref, scaled_ref, dy_ref, in_ref, ds_ref,
    ed_ref, fade_ref, skip_ref, b_ref, c_ref, dbw_ref, dcw_ref, dt_ref, dtg_ref, ldg_ref,
    step_ref, step_bias_ref, decay_ref,
    y_ref, grad_ref, dstep_ref, first_ref, wsum_ref,
    dact, ends, begins, shifted, net_sum, grow_sum, head_sum, picks, nets, grows, heads,
):
    at = pl.program_id(0)

    def conv_back(j, slot, dpre):
        lanes = lanes_at(j)
        first_ref[:, lanes] = dpre[:16].astype(BF16)
        shifted[slot, 8 : ROWS + 8, :] = dpre
        raw = raw_ref[:, lanes].astype(F32)
        before = halo_ref[8:16, lanes].astype(F32)
        grad = weight_ref[CONV - 1 : CONV, lanes] * dpre
        sums = []
        for k in range(CONV):
            moved = dpre
            if k < CONV - 1:
                moved = shifted[slot, 11 - k : ROWS + 11 - k, :]
                grad = grad + weight_ref[k : k + 1, lanes] * moved
            total = jnp.sum(raw * moved, 0, keepdims=True)
            if k < CONV - 1:
                edge = before * shifted[slot, 3 - k : 11 - k, :]
                total = total + jnp.sum(edge, 0, keepdims=True)
            sums.append(total)
        sums.append(jnp.sum(dpre, 0, keepdims=True))
        sums.append(jnp.zeros((3, 128), F32))
        grad_ref[:, lanes] = grad.astype(BF16)
        wsum_ref[:, lanes] = jnp.concatenate(sums, 0)

    @pl.when(at == 0)
    def _():
        shifted[:, 0:8, :] = jnp.zeros((2, 8, 128), F32)
        shifted[:, ROWS + 8 : ROWS + 16, :] = jnp.zeros((2, 8, 128), F32)
        picks[...] = head_picks()

    @pl.when(at < GROUPS)
    def _():
        group = at
        b = b_ref[...]
        c = c_ref[...]
        fades = fade_ref[pl.ds(group, 1), :]
        skips = skip_ref[pl.ds(group, 1), :]
        low = low_half()
        for j in range(PAIRS):
            lanes = lanes_at(j)
            ld = pair_lanes(ldg_ref[0], 2 * j, low)
            dt = pair_lanes(dtg_ref[0], 2 * j, low)
            act = act_ref[:, lanes].astype(F32)
            dy = dy_ref[:, lanes].astype(F32)
            scaled = scaled_ref[:, lanes].astype(F32)
            state = ed_ref[0, 0, :, lanes]
            dstate = ed_ref[1, 0, :, lanes]
            to_end = jnp.exp2(ld[ROWS - 1 : ROWS] - ld)
            from_start = jnp.exp2(ld)
            ends[:, lanes] = (scaled * to_end).astype(BF16)
            begins[:, lanes] = (dy * from_start).astype(BF16)
            inner = in_ref[:, lanes] + dot(c, state) * from_start
            dload = dot(b, dstate) * to_end
            dscaled = ds_ref[:, lanes] + dload
            skip = skips[:, lanes]
            y_ref[:, lanes] = (inner + skip * act).astype(BF16)
            grow = scaled * dscaled
            net = dy * inner - grow
            coarse = net.astype(BF16)
            nets[0, :, lanes] = coarse
            nets[1, :, lanes] = (net - coarse.astype(F32)).astype(BF16)
            grows[:, lanes] = grow.astype(BF16)
            ends_sum = jnp.sum(scaled * dload, 0, keepdims=True)
            ends_sum = ends_sum + fades[:, lanes] * jnp.sum(
                state.astype(F32) * dstate.astype(F32), 0, keepdims=True
            )
            skip_sum = jnp.sum(dy * act, 0, keepdims=True)
            heads[0:1, lanes] = ends_sum
            heads[1:2, lanes] = skip_sum
            conv_back(j, j % 2, (dt * dscaled + skip * dy) * slope_ref[:, lanes].astype(F32))

        net_sum[group] = dot(nets[0], picks[...]) + dot(nets[1], picks[...])
        grow_sum[group] = dot(grows[...], picks[...])
        rest = heads[...]
        total = jnp.zeros((8, HEADS), F32)
        for _ in range(3):
            piece = rest.astype(BF16)
            total = total + dot(piece, picks[...])
            rest = rest - piece.astype(F32)
        head_sum[group] = total
        here = lanes_at(group)
        dact[0, :, here] = dbw_ref[...] + dot_nt(ends[...], ed_ref[1, 0])
        dact[1, :, here] = dcw_ref[...] + dot_nt(begins[...], ed_ref[0, 0])

    @pl.when(at >= GROUPS)
    def _():
        for j in range(PAIRS):
            lanes = lanes_at(j)
            conv_back(j, j % 2, dact[at - GROUPS, :, lanes] * slope_ref[:, lanes].astype(F32))

    @pl.when(at == GROUPS)
    def _():
        lanes = lax.broadcasted_iota(jnp.int32, (ROWS, HEADS), 1)

        def of_heads(slabs):
            total = slabs[0]
            for group in range(1, GROUPS):
                moved = pltpu.roll(slabs[group], group * 2 * PAIRS, 1)
                here = lanes[: moved.shape[0]] >= group * 2 * PAIRS
                total = jnp.where(here, moved, total)
            return total

        dlog = of_heads(net_sum)
        extra = of_heads(head_sum)
        rows = lax.broadcasted_iota(jnp.int32, (ROWS, HEADS), 0)
        shift = 1
        while shift < ROWS:
            moved = pltpu.roll(dlog, ROWS - shift, 0)
            dlog = dlog + jnp.where(rows < ROWS - shift, moved, 0.0)
            shift *= 2
        dlog = dlog + extra[0:1]
        rates = -jnp.exp(decay_ref[...])
        dt = dt_ref[...]
        gate = jax.nn.sigmoid(step_ref[...].astype(F32) + step_bias_ref[...])
        dstep = (of_heads(grow_sum) / dt + rates * dlog) * gate
        dstep_ref[...] = dstep.astype(BF16)
        wsum_ref[5:6, 0:HEADS] = jnp.sum(dstep, 0, keepdims=True)
        wsum_ref[5:6, HEADS : 2 * HEADS] = rates * jnp.sum(dlog * dt, 0, keepdims=True)
        wsum_ref[5:6, 2 * HEADS : 3 * HEADS] = extra[1:2]


def total_kernel(wsum, first, out, after, parts, mine, sems, edge_sems):
    index = lax.axis_index("ctx")
    count = lax.axis_size("ctx")
    share = wsum.shape[1] // count
    ahead = lax.rem(index + 1, count)
    behind = lax.rem(index + count - 1, count)
    barrier = pltpu.get_barrier_semaphore()

    def greet(i, carry):
        other = lax.rem(index + i, count)
        pl.semaphore_signal(barrier, inc=1, device_id={"ctx": other}, device_id_type=MESH)
        return carry

    lax.fori_loop(1, count, greet, 0)
    pl.semaphore_wait(barrier, count - 1)

    edge = pltpu.make_async_remote_copy(
        src_ref=first, dst_ref=after, send_sem=edge_sems.at[0], recv_sem=edge_sems.at[1],
        device_id={"ctx": behind}, device_id_type=MESH,
    )
    edge.start()

    def columns(i):
        return pl.ds(pl.multiple_of(i * share, 128), share)

    def spread_out(i):
        other = lax.rem(index + i, count)
        return pltpu.make_async_remote_copy(
            src_ref=wsum.at[:, columns(other)], dst_ref=parts.at[i],
            send_sem=sems.at[0, 0, i], recv_sem=sems.at[0, 1, i],
            device_id={"ctx": other}, device_id_type=MESH,
        )

    def collect(i):
        other = lax.rem(index + i, count)
        return pltpu.make_async_remote_copy(
            src_ref=mine, dst_ref=out.at[:, columns(index)],
            send_sem=sems.at[1, 0, i], recv_sem=sems.at[1, 1, i],
            device_id={"ctx": other}, device_id_type=MESH,
        )

    def start_spread(i, carry):
        spread_out(i).start()
        return carry

    lax.fori_loop(1, count, start_spread, 0)
    mine[...] = wsum[:, columns(index)]

    def add(i, carry):
        spread_out(i).wait_recv()
        mine[...] += parts[i]
        return carry

    lax.fori_loop(1, count, add, 0)

    def start_collect(i, carry):
        collect(i).start()
        return carry

    lax.fori_loop(1, count, start_collect, 0)
    out[:, columns(index)] = mine[...]

    def end(i, carry):
        spread_out(i).wait_send()
        collect(i).wait()
        return carry

    lax.fori_loop(1, count, end, 0)
    edge.wait()


def edge_kernel(grad_ref, after_ref, weight_ref, total_ref, grad_out_ref, gw_ref, gv_ref, h0, h1, h2):
    last = lax.axis_index("ctx") == lax.axis_size("ctx") - 1
    after = jnp.where(last, 0.0, after_ref[0:8].astype(F32))
    rows = lax.broadcasted_iota(jnp.int32, after.shape, 0)
    more = jnp.zeros_like(after)
    for k in range(CONV - 1):
        moved = pltpu.roll(after, 5 + k, 0)
        more = more + jnp.where(rows >= 5 + k, weight_ref[k : k + 1] * moved, 0.0)
    more = jnp.concatenate([jnp.zeros_like(more), more], 0)
    grad_out_ref[...] = (grad_ref[...].astype(F32) + more).astype(BF16)
    gw_ref[...] = total_ref[0:CONV]
    gv_ref[...] = total_ref[CONV : CONV + 1]
    for place, ref in enumerate((h0, h1, h2)):
        start = INNER + place * HEADS
        ref[...] = total_ref[5:6, start : start + HEADS]


def params(**kw):
    return pltpu.CompilerParams(vmem_limit_bytes=VMEM_LIMIT, **kw)


sds = jax.ShapeDtypeStruct
VMEM = pl.BlockSpec(memory_space=pltpu.VMEM)


def whole(*shape):
    return pl.BlockSpec(shape, lambda g: (0,) * len(shape))


def columns_of(rows, pick, width=WIDTH):
    return pl.BlockSpec((rows, width), lambda g: (0, pick(g)))


def slab(pick):
    return pl.BlockSpec((1, ROWS, HEADS), lambda g: (pick(g), 0, 0))


def same(g):
    return g


def call_blocks(
    mixer_in, conv_weight, conv_bias, grad_out, step_raw, step_bias, decay_log, skip_gain
):
    def block(g):
        return jnp.where(g < BLOCKS, lax.rem(g + GROUPS, BLOCKS), GROUPS - 1)

    def first(g):
        return jnp.clip(g - 2, 0, GROUPS - 1)

    def second(g):
        return jnp.maximum(g - BLOCKS, 0)

    def either(g):
        return jnp.where(g < BLOCKS, jnp.maximum(g - 2, 0), g - BLOCKS)

    slabs = sds((GROUPS, ROWS, HEADS), F32)
    return pl.pallas_call(
        block_kernel,
        grid=(BLOCKS + GROUPS,),
        in_specs=[columns_of(ROWS, block), pl.BlockSpec(memory_space=pl.ANY)]
        + [columns_of(CONV, block), columns_of(1, block), columns_of(ROWS, either)]
        + [whole(ROWS, HEADS)]
        + [whole(1, HEADS)] * 3,
        out_specs=[columns_of(ROWS, block), columns_of(ROWS, block), columns_of(ROWS, first)]
        + [columns_of(ROWS, second)] * 2
        + [columns_of(ROWS, second, STATE)] * 2
        + [VMEM] * 7,
        out_shape=[sds((ROWS, CHANNELS), BF16)] * 2
        + [sds((ROWS, INNER), BF16)]
        + [sds((ROWS, INNER), F32)] * 2
        + [sds((ROWS, SPAN), F32)] * 2
        + [sds((2, CHUNKS, PIECE, WIDTH), BF16), sds((16, CHANNELS), BF16)]
        + [sds((GROUPS, WIDTH), F32)] * 2
        + [sds((ROWS, HEADS), F32), slabs, slabs],
        scratch_shapes=[
            pltpu.VMEM((16, CHANNELS), BF16),
            pltpu.VMEM((GROUPS, WIDTH), F32),
            pltpu.VMEM((CHUNKS, PIECE, WIDTH), BF16),
            pltpu.VMEM((HEADS, ROWS), F32),
            pltpu.VMEM((2, SPAN, ROWS), BF16),
            pltpu.VMEM((2, ROWS + 8, 128), F32),
            pltpu.VMEM((2, ROWS, SPAN), BF16),
            pltpu.VMEM((GROUPS, ROWS, WIDTH), BF16),
            pltpu.VMEM((2, CHUNKS, PIECE, WIDTH), BF16),
        ]
        + [pltpu.VMEM((CHUNKS, PIECE, WIDTH), BF16)] * 3
        + [
            pltpu.VMEM((GROUPS, WIDTH), F32),
            pltpu.VMEM((3, HALF, HALF), F32),
            pltpu.VMEM((3, HALF, HALF), F32),
            pltpu.SemaphoreType.DMA((2, 3, CHUNKS)),
            pltpu.SemaphoreType.DMA((4,)),
        ],
        compiler_params=params(collective_id=1, has_side_effects=True),
        name="blocks",
    )(
        mixer_in, mixer_in, conv_weight, conv_bias, grad_out, step_raw, step_bias, decay_log,
        skip_gain,
    )


def call_finish(
    mixer_in, halo, conv_weight, slope, act, scaled, grad_out, inner, dscaled, ed, fade, skip,
    dbw, dcw, dt, dtg, ldg, step_raw, step_bias, decay_log,
):
    def group(g):
        return jnp.minimum(g, GROUPS - 1)

    return pl.pallas_call(
        finish_kernel,
        grid=(BLOCKS,),
        in_specs=[columns_of(n, same) for n in (ROWS, 16, CONV, ROWS)]
        + [columns_of(ROWS, group)] * 5
        + [
            pl.BlockSpec((2, 1, STATE, WIDTH), lambda g: (0, group(g), 0, 0)),
            whole(GROUPS, WIDTH),
            whole(GROUPS, WIDTH),
        ]
        + [columns_of(ROWS, lambda g: INNER // STATE + group(g), STATE)]
        + [columns_of(ROWS, lambda g: (INNER + SPAN) // STATE + group(g), STATE)]
        + [columns_of(ROWS, group, STATE)] * 2
        + [whole(ROWS, HEADS), slab(group), slab(group)]
        + [whole(ROWS, HEADS), whole(1, HEADS), whole(1, HEADS)],
        out_specs=[columns_of(ROWS, group), columns_of(ROWS, same), whole(ROWS, HEADS)]
        + [columns_of(16, same), columns_of(8, same)],
        out_shape=[
            sds((ROWS, INNER), BF16),
            sds((ROWS, CHANNELS), BF16),
            sds((ROWS, HEADS), BF16),
            sds((16, CHANNELS), BF16),
            sds((8, CHANNELS), F32),
        ],
        scratch_shapes=[
            pltpu.VMEM((2, ROWS, SPAN), F32),
            pltpu.VMEM((ROWS, WIDTH), BF16),
            pltpu.VMEM((ROWS, WIDTH), BF16),
            pltpu.VMEM((2, ROWS + 16, 128), F32),
            pltpu.VMEM((GROUPS, ROWS, HEADS), F32),
            pltpu.VMEM((GROUPS, ROWS, HEADS), F32),
            pltpu.VMEM((GROUPS, 8, HEADS), F32),
            pltpu.VMEM((WIDTH, HEADS), BF16),
            pltpu.VMEM((2, ROWS, WIDTH), BF16),
            pltpu.VMEM((ROWS, WIDTH), BF16),
            pltpu.VMEM((8, WIDTH), F32),
        ],
        compiler_params=params(),
        name="finish",
    )(
        mixer_in, halo, conv_weight, slope, act, scaled, grad_out, inner, dscaled, ed, fade, skip,
        act, act, dbw, dcw, dt, dtg, ldg, step_raw, step_bias, decay_log,
    )


def call_total(wsum, first):
    return pl.pallas_call(
        total_kernel,
        in_specs=[VMEM, VMEM],
        out_specs=[VMEM, VMEM],
        out_shape=[sds((8, CHANNELS), F32), sds((16, CHANNELS), BF16)],
        scratch_shapes=[
            pltpu.VMEM((16, 8, CHANNELS // 16), F32),
            pltpu.VMEM((8, CHANNELS // 16), F32),
            pltpu.SemaphoreType.DMA((2, 2, 16)),
            pltpu.SemaphoreType.DMA((2,)),
        ],
        compiler_params=params(collective_id=2, has_side_effects=True),
        name="totals",
    )(wsum, first)


def call_edge(grad, after, conv_weight, total):
    row = pl.BlockSpec((16, CHANNELS), lambda g: (ROWS // 16 - 1, 0))
    heads = sds((1, HEADS), F32)
    return pl.pallas_call(
        edge_kernel,
        grid=(1,),
        in_specs=[row, whole(16, CHANNELS), whole(CONV, CHANNELS), whole(8, CHANNELS)],
        out_specs=[row, whole(CONV, CHANNELS), whole(1, CHANNELS)] + [whole(1, HEADS)] * 3,
        out_shape=[sds((ROWS, CHANNELS), BF16), sds((CONV, CHANNELS), F32), sds((1, CHANNELS), F32)]
        + [heads] * 3,
        input_output_aliases={0: 0},
        compiler_params=params(),
        name="edge",
    )(grad, after, conv_weight, total)


def on_device(
    mixer_in, step_raw, step_bias, decay_log, skip_gain, conv_weight, conv_bias, grad_out
):
    step_bias, decay_log = step_bias[None], decay_log[None]
    act, slope, scaled, inner, dscaled, dbw, dcw, ed, halo, fade, skip, dt, dtg, ldg = call_blocks(
        mixer_in, conv_weight, conv_bias[None], grad_out, step_raw, step_bias, decay_log,
        skip_gain[None],
    )
    y, grad, dstep, first, wsum = call_finish(
        mixer_in, halo, conv_weight, slope, act, scaled, grad_out, inner, dscaled,
        ed.reshape(2, GROUPS, STATE, WIDTH), fade, skip, dbw, dcw, dt, dtg, ldg,
        step_raw, step_bias, decay_log,
    )
    total, after = call_total(wsum, first)
    grad, gw, gv, h0, h1, h2 = call_edge(grad, after, conv_weight, total)
    return (y, grad, dstep, gw, gv[0], h0[0], h1[0], h2[0])


def solution(mesh):
    rows = P(("dp", "ctx"), None)
    in_specs = (rows, rows, P(), P(), P(), P(), P(), rows)
    out_specs = (rows, rows, rows, P("dp", None), P("dp"), P("dp"), P("dp"), P("dp"))
    return jax.shard_map(
        on_device, mesh=mesh, in_specs=in_specs, out_specs=out_specs, check_vma=False
    )
```

```python
import functools
import math

import jax
import jax.numpy as jnp
from jax import lax
from jax.experimental import pallas as pl
from jax.experimental.pallas import tpu as pltpu
from jax.sharding import PartitionSpec as P

HEADS = 128
HEAD_DIM = 64
GROUPS = 8
STATE = 128
CONV = 4
ROWS = 256
HALF = ROWS // 2
INNER = HEADS * HEAD_DIM
SPAN = GROUPS * STATE
CHANNELS = INNER + 2 * SPAN
WIDTH = INNER // GROUPS
PAIRS = WIDTH // 128
BLOCKS = CHANNELS // WIDTH
CHUNKS = 8
PIECE = STATE * GROUPS // CHUNKS
LAG = 2
LEAD = 2
LOG2E = math.log2(math.e)
F32 = jnp.float32
BF16 = jnp.bfloat16
MESH = pl.DeviceIdType.MESH
VMEM_LIMIT = 62 * 1024 * 1024


def dot(left, right):
    return jnp.dot(left, right, preferred_element_type=F32)


def dot_nt(left, right):
    return lax.dot_general(left, right, (((1,), (1,)), ((), ())), preferred_element_type=F32)


def dot_tn(left, right):
    return lax.dot_general(left, right, (((0,), (0,)), ((), ())), preferred_element_type=F32)


def pair_columns(values, first):
    return tuple(
        jnp.broadcast_to(values[:, first + i : first + i + 1], (ROWS, 128)) for i in range(2)
    )


def pair_lanes(values, first, low):
    return jnp.where(low, *pair_columns(values, first))


def head_picks():
    lanes = lax.broadcasted_iota(jnp.int32, (WIDTH, HEADS), 0)
    heads = lax.broadcasted_iota(jnp.int32, (WIDTH, HEADS), 1)
    return (heads == lanes // HEAD_DIM).astype(F32).astype(BF16)


def low_half():
    return lax.broadcasted_iota(jnp.int32, (ROWS, 128), 1) < HEAD_DIM


SECOND = BLOCKS
THIRD = BLOCKS + GROUPS
STEPS = THIRD + BLOCKS
SHARE = CHANNELS // 16
EDGE = 64
EARLY = (GROUPS - 2) * WIDTH // SHARE


def lanes_at(j):
    if isinstance(j, int):
        return slice(j * 128, (j + 1) * 128)
    return pl.ds(pl.multiple_of(j * 128, 128), 128)


def stack(*pieces):
    return jnp.concatenate(pieces, 0)


def beside(*pieces):
    return jnp.concatenate(pieces, 1)


def scores_of(group, j, dy_ref, scaled_ref, ldg_ref, ldt_ref, contact, dcontact, in_ref, ds_ref):
    lanes = lanes_at(j)
    first = group * (2 * PAIRS) + 2 * j
    low = low_half()
    rows = lax.broadcasted_iota(jnp.int32, (HALF, HALF), 0)
    causal = rows >= lax.broadcasted_iota(jnp.int32, (HALF, HALF), 1)
    dy = dy_ref[:, lanes]
    scaled = scaled_ref[:, lanes]
    zero = jnp.zeros_like(dy)
    dys = (jnp.where(low, dy, zero), jnp.where(low, zero, dy))
    xs = (jnp.where(low, scaled, zero), jnp.where(low, zero, scaled))
    top = dot_nt(stack(dys[0][:HALF], dys[1][:HALF]), scaled[:HALF])
    bottom = dot_nt(stack(dys[0][HALF:], dys[1][HALF:]), scaled)
    lds = pair_columns(ldg_ref[...], 2 * j)
    tiles = []
    for half in range(2):
        row = ldt_ref[pl.ds(first + half, 1), :]
        here = slice(HALF * half, HALF * half + HALF)
        for tile, mine, cols, grad in (
            (0, slice(0, HALF), slice(0, HALF), top[here]),
            (1, slice(HALF, ROWS), slice(0, HALF), bottom[here, :HALF]),
            (2, slice(HALF, ROWS), slice(HALF, ROWS), bottom[here, HALF:]),
        ):
            gap = lds[half][mine] - row[:, cols]
            if tile != 1:
                gap = jnp.where(causal, gap, -1e30)
            decay = jnp.exp2(gap)
            tiles.append((contact[tile] * decay).astype(BF16))
            dcontact[tile] += grad * decay
    in_ref[:HALF, lanes] = dot(beside(tiles[0], tiles[3]), stack(xs[0][:HALF], xs[1][:HALF]))
    in_ref[HALF:, lanes] = dot(beside(tiles[1], tiles[2], tiles[4], tiles[5]), stack(*xs))
    ds_ref[:HALF, lanes] = dot_tn(stack(tiles[0], tiles[1], tiles[3], tiles[4]), stack(*dys))
    ds_ref[HALF:, lanes] = dot_tn(stack(tiles[2], tiles[5]), stack(dys[0][HALF:], dys[1][HALF:]))


def start_tiles(b, c, contact, dcontact):
    contact[0] = dot_nt(c[:HALF], b[:HALF])
    both = dot_nt(c[HALF:], b)
    contact[1] = both[:, :HALF]
    contact[2] = both[:, HALF:]
    dcontact[...] = jnp.zeros_like(dcontact)


def end_tiles(b, c, dcontact, dbw_ref, dcw_ref):
    tiles = dcontact[...].astype(BF16)
    dbw_ref[:HALF] = dot_tn(stack(tiles[0], tiles[1]), c)
    dbw_ref[HALF:] = dot_tn(tiles[2], c[HALF:])
    dcw_ref[:HALF] = dot(tiles[0], b[:HALF])
    dcw_ref[HALF:] = dot(beside(tiles[1], tiles[2]), b)


def block_kernel(
    raw_ref, mixer_ref, weight_ref, bias_ref, dy_ref, step_ref, step_bias_ref, decay_ref, skip_ref,
    y_ref, grad_ref, dstep_ref, after_ref, total_ref,
    acts, slopes, xs, inners, dscales, fg, given, above, below, came,
    halo, fade, fades, skips, dts, dtg, ldg, ldt, shifted, contact, dcontact,
    ends, begins, nets, grows, heads, net_sum, grow_sum, head_sum, picks,
    wsum, first, after, parts, mine, total, dacts,
    sems, edge_sems, total_sems,
):
    at = pl.program_id(0)
    index = lax.axis_index("ctx")
    count = lax.axis_size("ctx")
    core, chip = lax.rem(index, 2), index // 2
    own = 1 - core
    partner = index + 1 - 2 * core
    ahead = lax.rem(index + 2, count)
    behind = lax.rem(index + count - 2, count)
    down = jnp.where(core == 1, ahead, behind)
    place = jnp.where(core == 1, chip, count // 2 - 1 - chip)
    has_up = place > 0
    has_down = place < count // 2 - 1
    following = lax.rem(index + 1, count)
    previous = lax.rem(index + count - 1, count)
    block = jnp.where(at < BLOCKS, lax.rem(at + GROUPS, BLOCKS), at - THIRD)

    def remote(src, dst, send, recv, to):
        return pltpu.make_async_remote_copy(
            src_ref=src, dst_ref=dst, send_sem=send, recv_sem=recv,
            device_id={"ctx": to}, device_id_type=MESH,
        )

    def copy(kind, q, src, dst, to):
        return remote(src, dst, sems.at[0, kind, q], sems.at[1, kind, q], to)

    def give(q):
        return copy(0, q, fg.at[core, q], given.at[q], partner)

    def pass_on(q):
        return copy(1, q, below.at[q], above.at[q], down)

    def share(q):
        return copy(2, q, above.at[q], came.at[q], partner)

    tail = mixer_ref.at[pl.ds(ROWS - 16, 16), :]
    x_cols, bc_cols = pl.ds(0, INNER), pl.ds(INNER, 2 * SPAN)

    def halo_copy(kind, cols):
        return remote(
            tail.at[:, cols], halo.at[:, cols],
            edge_sems.at[8 + 2 * kind], edge_sems.at[9 + 2 * kind], following,
        )


    def first_copy(kind, cols):
        return remote(
            first.at[:, cols], after.at[:, cols],
            edge_sems.at[4 + 2 * kind], edge_sems.at[5 + 2 * kind], previous,
        )

    def share_cols(i):
        return pl.ds(pl.multiple_of(i * SHARE, 128), SHARE)

    def part_copy(sender, to):
        return remote(
            wsum.at[:, share_cols(to)], parts.at[sender],
            total_sems.at[0, 0, to], total_sems.at[0, 1, sender], to,
        )

    def total_copy(sender, to):
        return remote(
            mine, total.at[:, share_cols(sender)],
            total_sems.at[1, 0, to], total_sems.at[1, 1, sender], to,
        )

    def others(body):
        def step(i, carry):
            body(lax.rem(index + i, count))
            return carry

        lax.fori_loop(1, count, step, 0)

    fade_copy = remote(fade, fades, edge_sems.at[2], edge_sems.at[3], partner)

    @pl.when(at == 0)
    def _():
        barrier = pltpu.get_barrier_semaphore()
        others(
            lambda other: pl.semaphore_signal(
                barrier, inc=1, device_id={"ctx": other}, device_id_type=MESH
            )
        )
        pl.semaphore_wait(barrier, count - 1)
        halo_copy(1, bc_cols).start()
        halo_copy(0, x_cols).start()

        dt = jax.nn.softplus(step_ref[...].astype(F32) + step_bias_ref[...])
        ld = dt * (-jnp.exp(decay_ref[...]) * LOG2E)
        rows = lax.broadcasted_iota(jnp.int32, (ROWS, HEADS), 0)
        shift = 1
        while shift < ROWS:
            ld = ld + jnp.where(rows >= shift, pltpu.roll(ld, shift, 0), 0.0)
            shift *= 2
        dts[...] = dt
        ldt[...] = ld.T
        picks[...] = head_picks()
        wsum[...] = jnp.zeros_like(wsum)
        for group in range(GROUPS):
            shift = (HEADS - group * 2 * PAIRS) % HEADS
            dtg[group] = pltpu.roll(dt, shift, 1) if shift else dt
            ldg[group] = pltpu.roll(ld, shift, 1) if shift else ld
        low = lax.broadcasted_iota(jnp.int32, (1, 128), 1) < HEAD_DIM
        for row, out in ((jnp.exp2(ld[ROWS - 1 : ROWS]), fade), (skip_ref[...], skips)):
            for group in range(GROUPS):
                for j in range(PAIRS):
                    at_head = group * 2 * PAIRS + 2 * j
                    pair = [
                        jnp.broadcast_to(row[:, at_head + i : at_head + i + 1], (1, 128))
                        for i in range(2)
                    ]
                    out[group : group + 1, lanes_at(j)] = jnp.where(low, *pair)
        fade_copy.start()

        @pl.when(jnp.logical_not(has_up))
        def _():
            above[...] = jnp.zeros_like(above)

        halo_copy(1, bc_cols).wait()

        @pl.when(index == 0)
        def _():
            halo[:, INNER:] = jnp.zeros((16, 2 * SPAN), BF16)

    @pl.when(at == 2)
    def _():
        halo_copy(0, x_cols).wait()

        @pl.when(index == 0)
        def _():
            halo[:, :INNER] = jnp.zeros((16, INNER), BF16)

        fade_copy.wait()

    def serve(q):
        block = q // (CHUNKS // GROUPS)
        mine = fade[pl.ds(block, 1), :]
        theirs = fades[pl.ds(block, 1), :]
        give(q).wait_recv()
        got = given[q].astype(F32)

        @pl.when(has_up)
        def _():
            pass_on(q).wait_recv()

        here = got + theirs * above[q].astype(F32)

        @pl.when(has_down)
        def _():
            below[q] = (fg[own, q].astype(F32) + mine * here).astype(BF16)
            pass_on(q).start()

        share(q).start()
        fg[own, q] = here.astype(BF16)

    def serve_at(slot):
        q = slot - LEAD - LAG * place
        pl.when(jnp.logical_and(q >= 0, q < CHUNKS))(functools.partial(serve, q))

    def turned_at(group):
        row, lane = (group // 4) * STATE, lax.rem(group, 4) * ROWS
        return pl.ds(pl.multiple_of(row, STATE), STATE), pl.ds(pl.multiple_of(lane, ROWS), ROWS)

    def block_lanes(j):
        return pl.ds(pl.multiple_of(block * WIDTH + j * 128, 128), 128)

    def conv(j):
        lanes = lanes_at(j)
        slot = j % 2
        shifted[slot, 0:8, :] = halo[8:16, block_lanes(j)].astype(F32)
        raw = raw_ref[:, lanes].astype(F32)
        shifted[slot, 8 : ROWS + 8, :] = raw
        pre = bias_ref[:, lanes] + weight_ref[CONV - 1 : CONV, lanes] * raw
        for k in range(CONV - 1):
            pre = pre + weight_ref[k : k + 1, lanes] * shifted[slot, 5 + k : ROWS + 5 + k, :]
        gate = 1.0 / (1.0 + jnp.exp(-pre))
        act = pre * gate
        slopes[block, :, lanes] = (gate + act * (1.0 - gate)).astype(BF16)
        rounded = act.astype(BF16)
        acts[block, :, lanes] = rounded
        return rounded

    @pl.when(at < 2)
    def _():
        for j in range(PAIRS):
            act = conv(j)
            nets[(at,) + turned_at(j)] = act.T

    pl.when(jnp.logical_and(at >= 2, at < STEPS - 2))(lambda: serve_at(at - 2))

    @pl.when(jnp.logical_and(at >= 2, at < SECOND))
    def _():
        group = at - 2
        mine = turned_at(group)
        per = CHUNKS // GROUPS
        low = low_half()
        for j in range(PAIRS):
            lanes = lanes_at(j)
            act = conv(j)
            ld = pair_lanes(ldg[group], 2 * j, low)
            dt = pair_lanes(dtg[group], 2 * j, low)
            last = ld[ROWS - 1 : ROWS]
            scaled = (act.astype(F32) * dt).astype(BF16)
            xs[group, :, lanes] = scaled
            ends = (scaled.astype(F32) * jnp.exp2(last - ld)).astype(BF16)
            begins = (dy_ref[:, lanes].astype(F32) * jnp.exp2(ld)).astype(BF16)
            for kind, piece in ((0, ends), (1, begins)):
                state = dot(nets[(kind,) + mine], piece).astype(BF16)
                fg[kind, pl.ds(group * per, per), :, lanes] = state.reshape(per, PIECE, 128)

        def start_give(r, carry):
            give(group * per + r).start()
            return carry

        lax.fori_loop(0, per, start_give, 0)

    @pl.when(jnp.logical_and(at >= SECOND, at < THIRD))
    def _():
        group = at - SECOND
        where = lanes_at(group)
        b = acts[GROUPS, :, where]
        c = acts[GROUPS + 1, :, where]
        start_tiles(b, c, contact, dcontact)
        for j in range(PAIRS):
            scores_of(
                group, j, dy_ref, xs.at[group], ldg.at[group], ldt, contact, dcontact,
                inners.at[group], dscales.at[group],
            )
        end_tiles(b, c, dcontact, dacts.at[0, :, where], dacts.at[1, :, where])

    def conv_back(j, slot, dpre):
        lanes = lanes_at(j)
        here = block_lanes(j)
        first[:, here] = dpre[:16].astype(BF16)
        shifted[slot, 8 : ROWS + 8, :] = dpre
        raw = raw_ref[:, lanes].astype(F32)
        before = halo[8:16, here].astype(F32)
        grad = weight_ref[CONV - 1 : CONV, lanes] * dpre
        sums = []
        for k in range(CONV):
            moved = dpre
            if k < CONV - 1:
                moved = shifted[slot, 11 - k : ROWS + 11 - k, :]
                grad = grad + weight_ref[k : k + 1, lanes] * moved
            total = jnp.sum(raw * moved, 0, keepdims=True)
            if k < CONV - 1:
                edge = before * shifted[slot, 3 - k : 11 - k, :]
                total = total + jnp.sum(edge, 0, keepdims=True)
            sums.append(total)
        sums.append(jnp.sum(dpre, 0, keepdims=True))
        sums.append(jnp.zeros((3, 128), F32))
        grad_ref[:, lanes] = grad.astype(BF16)
        wsum[:, here] = jnp.concatenate(sums, 0)

    @pl.when(at == 1)
    def _():
        shifted[:, 0:8, :] = jnp.zeros((2, 8, 128), F32)
        shifted[:, ROWS + 8 : ROWS + 16, :] = jnp.zeros((2, 8, 128), F32)

    def add_up():
        mine[...] = wsum[:, share_cols(index)]

        def add(sender):
            part_copy(sender, index).wait_recv()
            mine[...] += parts[sender]

        others(add)
        others(lambda other: total_copy(index, other).start())
        total[:, share_cols(index)] = mine[...]

    pl.when(jnp.logical_and(at == THIRD + GROUPS - 1, index < EARLY))(add_up)

    @pl.when(jnp.logical_and(at >= THIRD, at < THIRD + GROUPS))
    def _():
        group = at - THIRD
        per = CHUNKS // GROUPS
        for r in range(per):
            q = group * per + r
            share(q).wait_recv()
            give(q).wait_send()
            fg[core, q] = came[q]
        where = lanes_at(group)
        b = acts[GROUPS, :, where]
        c = acts[GROUPS + 1, :, where]
        fade_row = fade[pl.ds(group, 1), :]
        skip_row = skips[pl.ds(group, 1), :]
        low = low_half()
        for j in range(PAIRS):
            lanes = lanes_at(j)
            ld = pair_lanes(ldg[group], 2 * j, low)
            dt = pair_lanes(dtg[group], 2 * j, low)
            act = acts[group, :, lanes].astype(F32)
            dy = dy_ref[:, lanes].astype(F32)
            scaled = xs[group, :, lanes].astype(F32)
            state = fg[0, pl.ds(group * per, per), :, lanes].reshape(STATE, 128)
            dstate = fg[1, pl.ds(group * per, per), :, lanes].reshape(STATE, 128)
            to_end = jnp.exp2(ld[ROWS - 1 : ROWS] - ld)
            from_start = jnp.exp2(ld)
            ends[:, lanes] = (scaled * to_end).astype(BF16)
            begins[:, lanes] = (dy * from_start).astype(BF16)
            inner = inners[group, :, lanes] + dot(c, state) * from_start
            dload = dot(b, dstate) * to_end
            dscaled = dscales[group, :, lanes] + dload
            skip = skip_row[:, lanes]
            y_ref[:, lanes] = (inner + skip * act).astype(BF16)
            grow = scaled * dscaled
            net = dy * inner - grow
            coarse = net.astype(BF16)
            nets[0, :, lanes] = coarse
            nets[1, :, lanes] = (net - coarse.astype(F32)).astype(BF16)
            grows[:, lanes] = grow.astype(BF16)
            ends_sum = jnp.sum(scaled * dload, 0, keepdims=True)
            ends_sum = ends_sum + fade_row[:, lanes] * jnp.sum(
                state.astype(F32) * dstate.astype(F32), 0, keepdims=True
            )
            skip_sum = jnp.sum(dy * act, 0, keepdims=True)
            heads[0:1, lanes] = ends_sum
            heads[1:2, lanes] = skip_sum
            conv_back(j, j % 2, (dt * dscaled + skip * dy) * slopes[block, :, lanes].astype(F32))

        net_sum[group] = dot(nets[0], picks[...]) + dot(nets[1], picks[...])
        grow_sum[group] = dot(grows[...], picks[...])
        rest = heads[...]
        total = jnp.zeros((8, HEADS), F32)
        for _ in range(3):
            piece = rest.astype(BF16)
            total = total + dot(piece, picks[...])
            rest = rest - piece.astype(F32)
        head_sum[group] = total
        state = fg[0, pl.ds(group * per, per)].reshape(STATE, WIDTH)
        dstate = fg[1, pl.ds(group * per, per)].reshape(STATE, WIDTH)
        dacts[0, :, where] += dot_nt(ends[...], dstate)
        dacts[1, :, where] += dot_nt(begins[...], state)

    @pl.when(at >= THIRD + GROUPS)
    def _():
        for j in range(PAIRS):
            lanes = lanes_at(j)
            conv_back(j, j % 2, dacts[at - THIRD - GROUPS, :, lanes] * slopes[block, :, lanes].astype(F32))

    @pl.when(at == THIRD + GROUPS)
    def _():
        lanes = lax.broadcasted_iota(jnp.int32, (ROWS, HEADS), 1)

        def of_heads(slabs):
            total = slabs[0]
            for group in range(1, GROUPS):
                moved = pltpu.roll(slabs[group], group * 2 * PAIRS, 1)
                here = lanes[: moved.shape[0]] >= group * 2 * PAIRS
                total = jnp.where(here, moved, total)
            return total

        dlog = of_heads(net_sum)
        extra = of_heads(head_sum)
        rows = lax.broadcasted_iota(jnp.int32, (ROWS, HEADS), 0)
        shift = 1
        while shift < ROWS:
            moved = pltpu.roll(dlog, ROWS - shift, 0)
            dlog = dlog + jnp.where(rows < ROWS - shift, moved, 0.0)
            shift *= 2
        dlog = dlog + extra[0:1]
        rates = -jnp.exp(decay_ref[...])
        dt = dts[...]
        gate = jax.nn.sigmoid(step_ref[...].astype(F32) + step_bias_ref[...])
        dstep = (of_heads(grow_sum) / dt + rates * dlog) * gate
        dstep_ref[...] = dstep.astype(BF16)
        wsum[5:6, INNER : INNER + HEADS] = jnp.sum(dstep, 0, keepdims=True)
        wsum[5:6, INNER + HEADS : INNER + 2 * HEADS] = rates * jnp.sum(dlog * dt, 0, keepdims=True)
        wsum[5:6, INNER + 2 * HEADS : INNER + 3 * HEADS] = extra[1:2]

    @pl.when(at >= THIRD)
    def _():
        def start_part(i, carry):
            pl.when(i != index)(lambda: part_copy(index, i).start())
            return carry

        k = at - THIRD
        lax.fori_loop(k * WIDTH // SHARE, (k + 1) * WIDTH // SHARE, start_part, 0)

    pl.when(at == THIRD + GROUPS - 1)(lambda: first_copy(0, x_cols).start())

    @pl.when(at == STEPS - 1)
    def _():
        first_copy(1, bc_cols).start()
        pl.when(index >= EARLY)(add_up)

        def finish(q, carry):
            @pl.when(has_down)
            def _():
                pass_on(q).wait_send()

            share(q).wait_send()
            return carry

        lax.fori_loop(0, CHUNKS, finish, 0)
        first_copy(0, x_cols).wait()
        first_copy(1, bc_cols).wait()
        after_ref[...] = after[...]

        def end(other):
            part_copy(index, other).wait_send()
            total_copy(index, other).wait_send()
            total_copy(other, index).wait_recv()

        others(end)
        total_ref[...] = total[...]


def edge_kernel(
    y_in, grad_in, dstep_in, after_ref, total_ref, weight_ref,
    y_out, grad_out, dstep_out, gw_ref, gv_ref, h0_ref, h1_ref, h2_ref,
    y_held, grad_held, sems,
):
    count = y_in.shape[0] // EDGE
    pairs = []
    for kind, (src, held, dst) in enumerate(((grad_in, grad_held, grad_out), (y_in, y_held, y_out))):
        for i in range(count):
            rows = pl.ds((count - 1 - i) * EDGE, EDGE)
            pairs.append(
                (
                    pltpu.make_async_copy(src.at[rows], held.at[rows], sems.at[0, kind, i]),
                    pltpu.make_async_copy(held.at[rows], dst.at[rows], sems.at[1, kind, i]),
                )
            )
    for fetch, _ in pairs:
        fetch.start()
    dstep_out[...] = dstep_in[...]
    gw_ref[...] = total_ref[0:CONV]
    gv_ref[...] = total_ref[CONV : CONV + 1]
    for place, ref in enumerate((h0_ref, h1_ref, h2_ref)):
        start = INNER + place * HEADS
        ref[...] = total_ref[5:6, start : start + HEADS]
    last = lax.axis_index("ctx") == lax.axis_size("ctx") - 1
    after = jnp.where(last, 0.0, after_ref[0:8].astype(F32))
    rows = lax.broadcasted_iota(jnp.int32, after.shape, 0)
    more = jnp.zeros_like(after)
    for k in range(CONV - 1):
        moved = pltpu.roll(after, 5 + k, 0)
        more = more + jnp.where(rows >= 5 + k, weight_ref[k : k + 1] * moved, 0.0)
    more = jnp.concatenate([jnp.zeros_like(more), more], 0)
    for i, (fetch, store) in enumerate(pairs):
        fetch.wait()
        if i == 0:
            tail = grad_held[ROWS - 16 :].astype(F32) + more
            grad_held[ROWS - 16 :] = tail.astype(BF16)
        store.start()
    for _, store in pairs:
        store.wait()


def params(**kw):
    return pltpu.CompilerParams(vmem_limit_bytes=VMEM_LIMIT, **kw)


sds = jax.ShapeDtypeStruct
VMEM = pl.BlockSpec(memory_space=pltpu.VMEM)


def whole(*shape):
    return pl.BlockSpec(shape, lambda g: (0,) * len(shape))


def columns_of(rows, pick, width=WIDTH):
    return pl.BlockSpec((rows, width), lambda g: (0, pick(g)))


def same(g):
    return g


def call_blocks(
    mixer_in, conv_weight, conv_bias, grad_out, step_raw, step_bias, decay_log, skip_gain
):
    def block(g):
        return jnp.where(g < BLOCKS, lax.rem(g + GROUPS, BLOCKS), jnp.maximum(g - THIRD, 0))

    def group(g):
        early = jnp.where(g < SECOND, jnp.maximum(g - 2, 0), g - SECOND)
        return jnp.where(g < THIRD, early, jnp.minimum(g - THIRD, GROUPS - 1))

    def y_block(g):
        return jnp.clip(g - THIRD, 0, GROUPS - 1)

    def grad_block(g):
        return jnp.maximum(g - THIRD, 0)

    def vmem(dtype, *shape):
        return pltpu.VMEM(shape, dtype)

    pieces = vmem(BF16, CHUNKS, PIECE, WIDTH)
    return pl.pallas_call(
        block_kernel,
        grid=(STEPS,),
        in_specs=[columns_of(ROWS, block), pl.BlockSpec(memory_space=pl.ANY)]
        + [columns_of(CONV, block), columns_of(1, block), columns_of(ROWS, group)]
        + [whole(ROWS, HEADS)]
        + [whole(1, HEADS)] * 3,
        out_specs=[columns_of(ROWS, y_block), columns_of(ROWS, grad_block)] + [VMEM] * 3,
        out_shape=[sds((ROWS, INNER), BF16), sds((ROWS, CHANNELS), BF16), sds((ROWS, HEADS), BF16)]
        + [sds((16, CHANNELS), BF16), sds((8, CHANNELS), F32)],
        scratch_shapes=[vmem(BF16, BLOCKS, ROWS, WIDTH)] * 2
        + [vmem(BF16, GROUPS, ROWS, WIDTH)]
        + [vmem(F32, GROUPS, ROWS, WIDTH)] * 2
        + [vmem(BF16, 2, CHUNKS, PIECE, WIDTH)]
        + [pieces] * 4
        + [vmem(BF16, 16, CHANNELS)]
        + [vmem(F32, GROUPS, WIDTH)] * 3
        + [vmem(F32, ROWS, HEADS), vmem(F32, GROUPS, ROWS, HEADS), vmem(F32, GROUPS, ROWS, HEADS)]
        + [vmem(F32, HEADS, ROWS), vmem(F32, 2, ROWS + 16, 128)]
        + [vmem(F32, 3, HALF, HALF)] * 2
        + [vmem(BF16, ROWS, WIDTH)] * 2
        + [vmem(BF16, 2, ROWS, WIDTH), vmem(BF16, ROWS, WIDTH), vmem(F32, 8, WIDTH)]
        + [vmem(F32, GROUPS, ROWS, HEADS)] * 2
        + [vmem(F32, GROUPS, 8, HEADS), vmem(BF16, WIDTH, HEADS)]
        + [vmem(F32, 8, CHANNELS), vmem(BF16, 16, CHANNELS), vmem(BF16, 16, CHANNELS)]
        + [vmem(F32, 16, 8, SHARE), vmem(F32, 8, SHARE), vmem(F32, 8, CHANNELS)]
        + [vmem(F32, 2, ROWS, SPAN)]
        + [
            pltpu.SemaphoreType.DMA((2, 3, CHUNKS)),
            pltpu.SemaphoreType.DMA((12,)),
            pltpu.SemaphoreType.DMA((2, 2, 16)),
        ],
        compiler_params=params(collective_id=1, has_side_effects=True),
        name="blocks",
    )(
        mixer_in, mixer_in, conv_weight, conv_bias, grad_out, step_raw, step_bias, decay_log,
        skip_gain,
    )


def call_edge(y, grad, dstep, after, total, conv_weight):
    far = pl.BlockSpec(memory_space=pl.ANY)
    heads = sds((1, HEADS), F32)
    return pl.pallas_call(
        edge_kernel,
        in_specs=[far, far] + [VMEM] * 4,
        out_specs=[far, far] + [VMEM] * 6,
        out_shape=[sds(y.shape, BF16), sds(grad.shape, BF16), sds(dstep.shape, BF16)]
        + [sds((CONV, CHANNELS), F32), sds((1, CHANNELS), F32)]
        + [heads] * 3,
        scratch_shapes=[
            pltpu.VMEM(y.shape, BF16),
            pltpu.VMEM(grad.shape, BF16),
            pltpu.SemaphoreType.DMA((2, 2, ROWS // EDGE)),
        ],
        compiler_params=params(),
        name="edge",
    )(y, grad, dstep, after, total, conv_weight)


def on_device(
    mixer_in, step_raw, step_bias, decay_log, skip_gain, conv_weight, conv_bias, grad_out
):
    y, grad, dstep, after, total = call_blocks(
        mixer_in, conv_weight, conv_bias[None], grad_out, step_raw, step_bias[None],
        decay_log[None], skip_gain[None],
    )
    y, grad, dstep, gw, gv, h0, h1, h2 = call_edge(y, grad, dstep, after, total, conv_weight)
    return (y, grad, dstep, gw, gv[0], h0[0], h1[0], h2[0])


def solution(mesh):
    rows = P(("dp", "ctx"), None)
    in_specs = (rows, rows, P(), P(), P(), P(), P(), rows)
    out_specs = (rows, rows, rows, P("dp", None), P("dp"), P("dp"), P("dp"), P("dp"))
    return jax.shard_map(
        on_device, mesh=mesh, in_specs=in_specs, out_specs=out_specs, check_vma=False
    )
```

```python
import functools
import math

import jax
import jax.numpy as jnp
from jax import lax
from jax.experimental import pallas as pl
from jax.experimental.pallas import tpu as pltpu
from jax.sharding import PartitionSpec as P

HEADS = 128
HEAD_DIM = 64
GROUPS = 8
STATE = 128
CONV = 4
ROWS = 256
HALF = ROWS // 2
INNER = HEADS * HEAD_DIM
SPAN = GROUPS * STATE
CHANNELS = INNER + 2 * SPAN
WIDTH = INNER // GROUPS
PAIRS = WIDTH // 128
BLOCKS = CHANNELS // WIDTH
CHUNKS = 8
PIECE = STATE * GROUPS // CHUNKS
LAG = 2
LEAD = 2
LOG2E = math.log2(math.e)
F32 = jnp.float32
BF16 = jnp.bfloat16
MESH = pl.DeviceIdType.MESH
VMEM_LIMIT = 62 * 1024 * 1024


def dot(left, right):
    return jnp.dot(left, right, preferred_element_type=F32)


def dot_nt(left, right):
    return lax.dot_general(left, right, (((1,), (1,)), ((), ())), preferred_element_type=F32)


def dot_tn(left, right):
    return lax.dot_general(left, right, (((0,), (0,)), ((), ())), preferred_element_type=F32)


def pair_columns(values, first):
    return tuple(
        jnp.broadcast_to(values[:, first + i : first + i + 1], (ROWS, 128)) for i in range(2)
    )


def pair_lanes(values, first, low):
    return jnp.where(low, *pair_columns(values, first))


def head_picks():
    lanes = lax.broadcasted_iota(jnp.int32, (WIDTH, HEADS), 0)
    heads = lax.broadcasted_iota(jnp.int32, (WIDTH, HEADS), 1)
    return (heads == lanes // HEAD_DIM).astype(F32).astype(BF16)


def low_half():
    return lax.broadcasted_iota(jnp.int32, (ROWS, 128), 1) < HEAD_DIM


SECOND = GROUPS
THIRD = 2 * GROUPS
STEPS = THIRD + BLOCKS
SHARE = INNER // 16
EDGE = 64
EARLY = (GROUPS - 2) * WIDTH // SHARE


def lanes_at(j):
    if isinstance(j, int):
        return slice(j * 128, (j + 1) * 128)
    return pl.ds(pl.multiple_of(j * 128, 128), 128)


def stack(*pieces):
    return jnp.concatenate(pieces, 0)


def beside(*pieces):
    return jnp.concatenate(pieces, 1)


def scores_of(group, j, dy_ref, scaled_ref, ldg_ref, ldt_ref, contact, dcontact, in_ref, ds_ref):
    lanes = lanes_at(j)
    first = group * (2 * PAIRS) + 2 * j
    low = low_half()
    rows = lax.broadcasted_iota(jnp.int32, (HALF, HALF), 0)
    causal = rows >= lax.broadcasted_iota(jnp.int32, (HALF, HALF), 1)
    dy = dy_ref[:, lanes]
    scaled = scaled_ref[:, lanes]
    zero = jnp.zeros_like(dy)
    dys = (jnp.where(low, dy, zero), jnp.where(low, zero, dy))
    xs = (jnp.where(low, scaled, zero), jnp.where(low, zero, scaled))
    top = dot_nt(stack(dys[0][:HALF], dys[1][:HALF]), scaled[:HALF])
    bottom = dot_nt(stack(dys[0][HALF:], dys[1][HALF:]), scaled)
    lds = pair_columns(ldg_ref[...], 2 * j)
    tiles = []
    for half in range(2):
        row = ldt_ref[pl.ds(first + half, 1), :]
        here = slice(HALF * half, HALF * half + HALF)
        for tile, mine, cols, grad in (
            (0, slice(0, HALF), slice(0, HALF), top[here]),
            (1, slice(HALF, ROWS), slice(0, HALF), bottom[here, :HALF]),
            (2, slice(HALF, ROWS), slice(HALF, ROWS), bottom[here, HALF:]),
        ):
            gap = lds[half][mine] - row[:, cols]
            if tile != 1:
                gap = jnp.where(causal, gap, -1e30)
            decay = jnp.exp2(gap)
            tiles.append((contact[tile] * decay).astype(BF16))
            dcontact[tile] += grad * decay
    in_ref[:HALF, lanes] = dot(beside(tiles[0], tiles[3]), stack(xs[0][:HALF], xs[1][:HALF]))
    in_ref[HALF:, lanes] = dot(beside(tiles[1], tiles[2], tiles[4], tiles[5]), stack(*xs))
    ds_ref[:HALF, lanes] = dot_tn(stack(tiles[0], tiles[1], tiles[3], tiles[4]), stack(*dys))
    ds_ref[HALF:, lanes] = dot_tn(stack(tiles[2], tiles[5]), stack(dys[0][HALF:], dys[1][HALF:]))


def start_tiles(b, c, contact, dcontact):
    contact[0] = dot_nt(c[:HALF], b[:HALF])
    both = dot_nt(c[HALF:], b)
    contact[1] = both[:, :HALF]
    contact[2] = both[:, HALF:]
    dcontact[...] = jnp.zeros_like(dcontact)


def end_tiles(b, c, dcontact, dbw_ref, dcw_ref):
    tiles = dcontact[...].astype(BF16)
    dbw_ref[:HALF] = dot_tn(stack(tiles[0], tiles[1]), c)
    dbw_ref[HALF:] = dot_tn(tiles[2], c[HALF:])
    dcw_ref[:HALF] = dot(tiles[0], b[:HALF])
    dcw_ref[HALF:] = dot(beside(tiles[1], tiles[2]), b)


def block_kernel(
    raw_ref, raw_b_ref, raw_c_ref, mixer_ref, weight_ref, weight_b_ref, weight_c_ref,
    bias_ref, bias_b_ref, bias_c_ref, dy_ref, step_ref, step_bias_ref, decay_ref, skip_ref,
    y_ref, grad_ref, dstep_ref, after_ref, total_ref,
    acts, slopes, xs, inners, dscales, fg, given, above, below, came,
    halo, fade, fades, skips, dts, dtg, ldg, ldt, shifted, contact, dcontact,
    ends, begins, nets, grows, heads, net_sum, grow_sum, head_sum, picks,
    wsum, first, after, parts_x, parts_bc, mine_x, mine_bc, total, dacts,
    sems, edge_sems, total_sems,
):
    at = pl.program_id(0)
    index = lax.axis_index("ctx")
    count = lax.axis_size("ctx")
    core, chip = lax.rem(index, 2), index // 2
    own = 1 - core
    partner = index + 1 - 2 * core
    ahead = lax.rem(index + 2, count)
    behind = lax.rem(index + count - 2, count)
    down = jnp.where(core == 1, ahead, behind)
    place = jnp.where(core == 1, chip, count // 2 - 1 - chip)
    has_up = place > 0
    has_down = place < count // 2 - 1
    following = lax.rem(index + 1, count)
    previous = lax.rem(index + count - 1, count)
    block = jnp.where(at < SECOND, at, at - THIRD)

    def remote(src, dst, send, recv, to):
        return pltpu.make_async_remote_copy(
            src_ref=src, dst_ref=dst, send_sem=send, recv_sem=recv,
            device_id={"ctx": to}, device_id_type=MESH,
        )

    def copy(kind, q, src, dst, to):
        return remote(src, dst, sems.at[0, kind, q], sems.at[1, kind, q], to)

    def give(q):
        return copy(0, q, fg.at[core, q], given.at[q], partner)

    def pass_on(q):
        return copy(1, q, below.at[q], above.at[q], down)

    def share(q):
        return copy(2, q, above.at[q], came.at[q], partner)

    tail = mixer_ref.at[pl.ds(ROWS - 16, 16), :]
    x_cols, bc_cols = pl.ds(0, INNER), pl.ds(INNER, 2 * SPAN)
    near_cols, far_cols = pl.ds(0, WIDTH), pl.ds(WIDTH, INNER - WIDTH)

    def halo_copy(kind, cols):
        return remote(
            tail.at[:, cols], halo.at[:, cols],
            edge_sems.at[8 + 2 * kind], edge_sems.at[9 + 2 * kind], following,
        )


    def first_copy(kind, cols):
        return remote(
            first.at[:, cols], after.at[:, cols],
            edge_sems.at[4 + 2 * kind], edge_sems.at[5 + 2 * kind], previous,
        )

    def share_cols(kind, i):
        if kind == 0:
            return pl.ds(pl.multiple_of(i * SHARE, 128), SHARE)
        return pl.ds(pl.multiple_of(INNER + i * 128, 128), 128)

    parts, mine = (parts_x, parts_bc), (mine_x, mine_bc)

    def part_copy(kind, sender, to):
        return remote(
            wsum.at[:, share_cols(kind, to)], parts[kind].at[sender],
            total_sems.at[kind, 0, 0, to], total_sems.at[kind, 0, 1, sender], to,
        )

    def total_copy(kind, sender, to):
        return remote(
            mine[kind], total.at[:, share_cols(kind, sender)],
            total_sems.at[kind, 1, 0, to], total_sems.at[kind, 1, 1, sender], to,
        )

    def others(body):
        def step(i, carry):
            body(lax.rem(index + i, count))
            return carry

        lax.fori_loop(1, count, step, 0)

    fade_copy = remote(fade, fades, edge_sems.at[2], edge_sems.at[3], partner)

    @pl.when(at == 0)
    def _():
        barrier = pltpu.get_barrier_semaphore()
        others(
            lambda other: pl.semaphore_signal(
                barrier, inc=1, device_id={"ctx": other}, device_id_type=MESH
            )
        )
        pl.semaphore_wait(barrier, count - 1)
        halo_copy(0, bc_cols).start()
        halo_copy(1, near_cols).start()
        halo_copy(2, far_cols).start()

        dt = jax.nn.softplus(step_ref[...].astype(F32) + step_bias_ref[...])
        ld = dt * (-jnp.exp(decay_ref[...]) * LOG2E)
        rows = lax.broadcasted_iota(jnp.int32, (ROWS, HEADS), 0)
        shift = 1
        while shift < ROWS:
            ld = ld + jnp.where(rows >= shift, pltpu.roll(ld, shift, 0), 0.0)
            shift *= 2
        dts[...] = dt
        ldt[...] = ld.T
        picks[...] = head_picks()
        wsum[...] = jnp.zeros_like(wsum)
        for group in range(GROUPS):
            shift = (HEADS - group * 2 * PAIRS) % HEADS
            dtg[group] = pltpu.roll(dt, shift, 1) if shift else dt
            ldg[group] = pltpu.roll(ld, shift, 1) if shift else ld
        low = lax.broadcasted_iota(jnp.int32, (1, 128), 1) < HEAD_DIM
        for row, out in ((jnp.exp2(ld[ROWS - 1 : ROWS]), fade), (skip_ref[...], skips)):
            for group in range(GROUPS):
                for j in range(PAIRS):
                    at_head = group * 2 * PAIRS + 2 * j
                    pair = [
                        jnp.broadcast_to(row[:, at_head + i : at_head + i + 1], (1, 128))
                        for i in range(2)
                    ]
                    out[group : group + 1, lanes_at(j)] = jnp.where(low, *pair)
        fade_copy.start()

        @pl.when(jnp.logical_not(has_up))
        def _():
            above[...] = jnp.zeros_like(above)

        halo_copy(0, bc_cols).wait()
        halo_copy(1, near_cols).wait()

        @pl.when(index == 0)
        def _():
            halo[:, INNER:] = jnp.zeros((16, 2 * SPAN), BF16)
            halo[:, :WIDTH] = jnp.zeros((16, WIDTH), BF16)

    @pl.when(at == 1)
    def _():
        halo_copy(2, far_cols).wait()

        @pl.when(index == 0)
        def _():
            halo[:, WIDTH:INNER] = jnp.zeros((16, INNER - WIDTH), BF16)

        fade_copy.wait()

    def serve(q):
        block = q // (CHUNKS // GROUPS)
        mine = fade[pl.ds(block, 1), :]
        theirs = fades[pl.ds(block, 1), :]
        give(q).wait_recv()
        got = given[q].astype(F32)

        @pl.when(has_up)
        def _():
            pass_on(q).wait_recv()

        here = got + theirs * above[q].astype(F32)

        @pl.when(has_down)
        def _():
            below[q] = (fg[own, q].astype(F32) + mine * here).astype(BF16)
            pass_on(q).start()

        share(q).start()
        fg[own, q] = here.astype(BF16)

    def serve_at(slot):
        q = slot - LEAD - LAG * place
        pl.when(jnp.logical_and(q >= 0, q < CHUNKS))(functools.partial(serve, q))

    def block_lanes(j):
        return pl.ds(pl.multiple_of(block * WIDTH + j * 128, 128), 128)

    def conv(raw_of, weight, bias, lanes, kind, here, halo_lanes, slot):
        shifted[slot, 0:8, :] = halo[8:16, halo_lanes].astype(F32)
        raw = raw_of[:, lanes].astype(F32)
        shifted[slot, 8 : ROWS + 8, :] = raw
        pre = bias[:, lanes] + weight[CONV - 1 : CONV, lanes] * raw
        for k in range(CONV - 1):
            pre = pre + weight[k : k + 1, lanes] * shifted[slot, 5 + k : ROWS + 5 + k, :]
        gate = 0.5 * jnp.tanh(0.5 * pre) + 0.5
        act = pre * gate
        slopes[kind, :, here] = (gate + act * (1.0 - gate)).astype(BF16)
        rounded = act.astype(BF16)
        acts[kind, :, here] = rounded
        return rounded

    pl.when(at < THIRD + GROUPS)(lambda: serve_at(at))

    @pl.when(at < SECOND)
    def _():
        group = at
        per = CHUNKS // GROUPS
        where = lanes_at(group)
        turned = []
        for kind, raw_of, weight, bias in (
            (0, raw_b_ref, weight_b_ref, bias_b_ref),
            (1, raw_c_ref, weight_c_ref, bias_c_ref),
        ):
            base = INNER + kind * SPAN + group * STATE
            halo_lanes = pl.ds(pl.multiple_of(base, STATE), STATE)
            act = conv(raw_of, weight, bias, slice(0, STATE), GROUPS + kind, where, halo_lanes, kind)
            turned.append(act.T)
        low = low_half()
        for j in range(PAIRS):
            lanes = lanes_at(j)
            act = conv(
                raw_ref, weight_ref, bias_ref, lanes, group, lanes, block_lanes(j), j % 2
            )
            ld = pair_lanes(ldg[group], 2 * j, low)
            dt = pair_lanes(dtg[group], 2 * j, low)
            last = ld[ROWS - 1 : ROWS]
            scaled = (act.astype(F32) * dt).astype(BF16)
            xs[group, :, lanes] = scaled
            ends = (scaled.astype(F32) * jnp.exp2(last - ld)).astype(BF16)
            begins = (dy_ref[:, lanes].astype(F32) * jnp.exp2(ld)).astype(BF16)
            if j % 2 == 0:
                held = (ends, begins)
                continue
            lanes = slice((j - 1) * 128, (j + 1) * 128)
            for kind, piece in ((0, ends), (1, begins)):
                state = dot(turned[kind], beside(held[kind], piece)).astype(BF16)
                fg[kind, pl.ds(group * per, per), :, lanes] = state.reshape(per, PIECE, 256)

        def start_give(r, carry):
            give(group * per + r).start()
            return carry

        lax.fori_loop(0, per, start_give, 0)

    @pl.when(jnp.logical_and(at >= SECOND, at < THIRD))
    def _():
        group = at - SECOND
        where = lanes_at(group)
        b = acts[GROUPS, :, where]
        c = acts[GROUPS + 1, :, where]
        start_tiles(b, c, contact, dcontact)
        for j in range(PAIRS):
            scores_of(
                group, j, dy_ref, xs.at[group], ldg.at[group], ldt, contact, dcontact,
                inners.at[group], dscales.at[group],
            )
        end_tiles(b, c, dcontact, dacts.at[0, :, where], dacts.at[1, :, where])

    def conv_back(j, slot, dpre):
        lanes = lanes_at(j)
        here = block_lanes(j)
        first[:, here] = dpre[:16].astype(BF16)
        shifted[slot, 8 : ROWS + 8, :] = dpre
        raw = raw_ref[:, lanes].astype(F32)
        before = halo[8:16, here].astype(F32)
        grad = weight_ref[CONV - 1 : CONV, lanes] * dpre
        sums = []
        for k in range(CONV):
            moved = dpre
            if k < CONV - 1:
                moved = shifted[slot, 11 - k : ROWS + 11 - k, :]
                grad = grad + weight_ref[k : k + 1, lanes] * moved
            total = jnp.sum(raw * moved, 0, keepdims=True)
            if k < CONV - 1:
                edge = before * shifted[slot, 3 - k : 11 - k, :]
                total = total + jnp.sum(edge, 0, keepdims=True)
            sums.append(total)
        sums.append(jnp.sum(dpre, 0, keepdims=True))
        sums.append(jnp.zeros((3, 128), F32))
        grad_ref[:, lanes] = grad.astype(BF16)
        wsum[:, here] = jnp.concatenate(sums, 0)

    @pl.when(at == SECOND)
    def _():
        shifted[:, 0:8, :] = jnp.zeros((2, 8, 128), F32)
        shifted[:, ROWS + 8 : ROWS + 16, :] = jnp.zeros((2, 8, 128), F32)

    def add_up(kind):
        held = mine[kind]
        held[...] = wsum[:, share_cols(kind, index)]

        def add(sender):
            part_copy(kind, sender, index).wait_recv()
            held[...] += parts[kind][sender]

        others(add)
        others(lambda other: total_copy(kind, index, other).start())
        total[:, share_cols(kind, index)] = held[...]

    @pl.when(jnp.logical_and(at == THIRD + GROUPS - 1, index < EARLY))
    def _():
        add_up(0)

    @pl.when(jnp.logical_and(at >= THIRD, at < THIRD + GROUPS))
    def _():
        group = at - THIRD
        per = CHUNKS // GROUPS
        for r in range(per):
            q = group * per + r
            share(q).wait_recv()
            give(q).wait_send()
            fg[core, q] = came[q]
        where = lanes_at(group)
        b = acts[GROUPS, :, where]
        c = acts[GROUPS + 1, :, where]
        fade_row = fade[pl.ds(group, 1), :]
        skip_row = skips[pl.ds(group, 1), :]
        low = low_half()
        for j in range(PAIRS):
            lanes = lanes_at(j)
            ld = pair_lanes(ldg[group], 2 * j, low)
            dt = pair_lanes(dtg[group], 2 * j, low)
            act = acts[group, :, lanes].astype(F32)
            dy = dy_ref[:, lanes].astype(F32)
            scaled = xs[group, :, lanes].astype(F32)
            state = fg[0, pl.ds(group * per, per), :, lanes].reshape(STATE, 128)
            dstate = fg[1, pl.ds(group * per, per), :, lanes].reshape(STATE, 128)
            to_end = jnp.exp2(ld[ROWS - 1 : ROWS] - ld)
            from_start = jnp.exp2(ld)
            ends[:, lanes] = (scaled * to_end).astype(BF16)
            begins[:, lanes] = (dy * from_start).astype(BF16)
            inner = inners[group, :, lanes] + dot(c, state) * from_start
            dload = dot(b, dstate) * to_end
            dscaled = dscales[group, :, lanes] + dload
            skip = skip_row[:, lanes]
            y_ref[:, lanes] = (inner + skip * act).astype(BF16)
            grow = scaled * dscaled
            net = dy * inner - grow
            coarse = net.astype(BF16)
            nets[0, :, lanes] = coarse
            nets[1, :, lanes] = (net - coarse.astype(F32)).astype(BF16)
            grows[:, lanes] = grow.astype(BF16)
            ends_sum = jnp.sum(scaled * dload, 0, keepdims=True)
            ends_sum = ends_sum + fade_row[:, lanes] * jnp.sum(
                state.astype(F32) * dstate.astype(F32), 0, keepdims=True
            )
            skip_sum = jnp.sum(dy * act, 0, keepdims=True)
            heads[0:1, lanes] = ends_sum
            heads[1:2, lanes] = skip_sum
            conv_back(j, j % 2, (dt * dscaled + skip * dy) * slopes[block, :, lanes].astype(F32))

        net_sum[group] = dot(nets[0], picks[...]) + dot(nets[1], picks[...])
        grow_sum[group] = dot(grows[...], picks[...])
        rest = heads[...]
        total = jnp.zeros((8, HEADS), F32)
        for _ in range(3):
            piece = rest.astype(BF16)
            total = total + dot(piece, picks[...])
            rest = rest - piece.astype(F32)
        head_sum[group] = total
        state = fg[0, pl.ds(group * per, per)].reshape(STATE, WIDTH)
        dstate = fg[1, pl.ds(group * per, per)].reshape(STATE, WIDTH)
        dacts[0, :, where] += dot_nt(ends[...], dstate)
        dacts[1, :, where] += dot_nt(begins[...], state)

    @pl.when(at >= THIRD + GROUPS)
    def _():
        for j in range(PAIRS):
            lanes = lanes_at(j)
            conv_back(j, j % 2, dacts[at - THIRD - GROUPS, :, lanes] * slopes[block, :, lanes].astype(F32))

    @pl.when(at == THIRD + GROUPS)
    def _():
        lanes = lax.broadcasted_iota(jnp.int32, (ROWS, HEADS), 1)

        def of_heads(slabs):
            total = slabs[0]
            for group in range(1, GROUPS):
                moved = pltpu.roll(slabs[group], group * 2 * PAIRS, 1)
                here = lanes[: moved.shape[0]] >= group * 2 * PAIRS
                total = jnp.where(here, moved, total)
            return total

        dlog = of_heads(net_sum)
        extra = of_heads(head_sum)
        rows = lax.broadcasted_iota(jnp.int32, (ROWS, HEADS), 0)
        shift = 1
        while shift < ROWS:
            moved = pltpu.roll(dlog, ROWS - shift, 0)
            dlog = dlog + jnp.where(rows < ROWS - shift, moved, 0.0)
            shift *= 2
        dlog = dlog + extra[0:1]
        rates = -jnp.exp(decay_ref[...])
        dt = dts[...]
        gate = jax.nn.sigmoid(step_ref[...].astype(F32) + step_bias_ref[...])
        dstep = (of_heads(grow_sum) / dt + rates * dlog) * gate
        dstep_ref[...] = dstep.astype(BF16)
        wsum[5:6, INNER : INNER + HEADS] = jnp.sum(dstep, 0, keepdims=True)
        wsum[5:6, INNER + HEADS : INNER + 2 * HEADS] = rates * jnp.sum(dlog * dt, 0, keepdims=True)
        wsum[5:6, INNER + 2 * HEADS : INNER + 3 * HEADS] = extra[1:2]

    @pl.when(at >= THIRD)
    def _():
        def start_part(kind, i, carry):
            pl.when(i != index)(lambda: part_copy(kind, index, i).start())
            return carry

        @pl.when(at < THIRD + GROUPS)
        def _():
            k = (at - THIRD) * (WIDTH // SHARE)
            lax.fori_loop(k, k + WIDTH // SHARE, functools.partial(start_part, 0), 0)

        @pl.when(at >= THIRD + GROUPS)
        def _():
            k = (at - THIRD - GROUPS) * GROUPS
            lax.fori_loop(k, k + GROUPS, functools.partial(start_part, 1), 0)

    pl.when(at == THIRD + GROUPS - 1)(lambda: first_copy(0, x_cols).start())

    @pl.when(at == STEPS - 1)
    def _():
        first_copy(1, bc_cols).start()
        pl.when(index >= EARLY)(lambda: add_up(0))
        add_up(1)

        def finish(q, carry):
            @pl.when(has_down)
            def _():
                pass_on(q).wait_send()

            share(q).wait_send()
            return carry

        lax.fori_loop(0, CHUNKS, finish, 0)
        first_copy(0, x_cols).wait()
        first_copy(1, bc_cols).wait()
        after_ref[...] = after[...]

        def end(other):
            for kind in range(2):
                part_copy(kind, index, other).wait_send()
                total_copy(kind, index, other).wait_send()
                total_copy(kind, other, index).wait_recv()

        others(end)
        total_ref[...] = total[...]


def edge_kernel(
    y_in, grad_in, dstep_in, after_ref, total_ref, weight_ref,
    y_out, grad_out, dstep_out, gw_ref, gv_ref, h0_ref, h1_ref, h2_ref,
    y_held, grad_held, sems,
):
    count = y_in.shape[0] // EDGE
    pairs = []
    for kind, (src, held, dst) in enumerate(((grad_in, grad_held, grad_out), (y_in, y_held, y_out))):
        for i in range(count):
            rows = pl.ds((count - 1 - i) * EDGE, EDGE)
            pairs.append(
                (
                    pltpu.make_async_copy(src.at[rows], held.at[rows], sems.at[0, kind, i]),
                    pltpu.make_async_copy(held.at[rows], dst.at[rows], sems.at[1, kind, i]),
                )
            )
    for fetch, _ in pairs:
        fetch.start()
    dstep_out[...] = dstep_in[...]
    gw_ref[...] = total_ref[0:CONV]
    gv_ref[...] = total_ref[CONV : CONV + 1]
    for place, ref in enumerate((h0_ref, h1_ref, h2_ref)):
        start = INNER + place * HEADS
        ref[...] = total_ref[5:6, start : start + HEADS]
    last = lax.axis_index("ctx") == lax.axis_size("ctx") - 1
    after = jnp.where(last, 0.0, after_ref[0:8].astype(F32))
    rows = lax.broadcasted_iota(jnp.int32, after.shape, 0)
    more = jnp.zeros_like(after)
    for k in range(CONV - 1):
        moved = pltpu.roll(after, 5 + k, 0)
        more = more + jnp.where(rows >= 5 + k, weight_ref[k : k + 1] * moved, 0.0)
    more = jnp.concatenate([jnp.zeros_like(more), more], 0)
    for i, (fetch, store) in enumerate(pairs):
        fetch.wait()
        if i == 0:
            tail = grad_held[ROWS - 16 :].astype(F32) + more
            grad_held[ROWS - 16 :] = tail.astype(BF16)
        store.start()
    for _, store in pairs:
        store.wait()


def params(**kw):
    return pltpu.CompilerParams(vmem_limit_bytes=VMEM_LIMIT, **kw)


sds = jax.ShapeDtypeStruct
VMEM = pl.BlockSpec(memory_space=pltpu.VMEM)


def whole(*shape):
    return pl.BlockSpec(shape, lambda g: (0,) * len(shape))


def columns_of(rows, pick, width=WIDTH):
    return pl.BlockSpec((rows, width), lambda g: (0, pick(g)))


def same(g):
    return g


def call_blocks(
    mixer_in, conv_weight, conv_bias, grad_out, step_raw, step_bias, decay_log, skip_gain
):
    def block(g):
        return jnp.where(g < SECOND, g, jnp.maximum(g - THIRD, 0))

    def group(g):
        early = jnp.where(g < SECOND, g, g - SECOND)
        return jnp.where(g < THIRD, early, jnp.minimum(g - THIRD, GROUPS - 1))

    def b_block(g):
        return INNER // STATE + jnp.minimum(g, GROUPS - 1)

    def c_block(g):
        return (INNER + SPAN) // STATE + jnp.minimum(g, GROUPS - 1)

    def three(rows):
        return [
            columns_of(rows, block),
            columns_of(rows, b_block, STATE),
            columns_of(rows, c_block, STATE),
        ]

    def y_block(g):
        return jnp.clip(g - THIRD, 0, GROUPS - 1)

    def grad_block(g):
        return jnp.maximum(g - THIRD, 0)

    def vmem(dtype, *shape):
        return pltpu.VMEM(shape, dtype)

    pieces = vmem(BF16, CHUNKS, PIECE, WIDTH)
    return pl.pallas_call(
        block_kernel,
        grid=(STEPS,),
        in_specs=three(ROWS)
        + [pl.BlockSpec(memory_space=pl.ANY)]
        + three(CONV)
        + three(1)
        + [columns_of(ROWS, group)]
        + [whole(ROWS, HEADS)]
        + [whole(1, HEADS)] * 3,
        out_specs=[columns_of(ROWS, y_block), columns_of(ROWS, grad_block)] + [VMEM] * 3,
        out_shape=[sds((ROWS, INNER), BF16), sds((ROWS, CHANNELS), BF16), sds((ROWS, HEADS), BF16)]
        + [sds((16, CHANNELS), BF16), sds((8, CHANNELS), F32)],
        scratch_shapes=[vmem(BF16, BLOCKS, ROWS, WIDTH)] * 2
        + [vmem(BF16, GROUPS, ROWS, WIDTH)]
        + [vmem(F32, GROUPS, ROWS, WIDTH)] * 2
        + [vmem(BF16, 2, CHUNKS, PIECE, WIDTH)]
        + [pieces] * 4
        + [vmem(BF16, 16, CHANNELS)]
        + [vmem(F32, GROUPS, WIDTH)] * 3
        + [vmem(F32, ROWS, HEADS), vmem(F32, GROUPS, ROWS, HEADS), vmem(F32, GROUPS, ROWS, HEADS)]
        + [vmem(F32, HEADS, ROWS), vmem(F32, 2, ROWS + 16, 128)]
        + [vmem(F32, 3, HALF, HALF)] * 2
        + [vmem(BF16, ROWS, WIDTH)] * 2
        + [vmem(BF16, 2, ROWS, WIDTH), vmem(BF16, ROWS, WIDTH), vmem(F32, 8, WIDTH)]
        + [vmem(F32, GROUPS, ROWS, HEADS)] * 2
        + [vmem(F32, GROUPS, 8, HEADS), vmem(BF16, WIDTH, HEADS)]
        + [vmem(F32, 8, CHANNELS), vmem(BF16, 16, CHANNELS), vmem(BF16, 16, CHANNELS)]
        + [vmem(F32, 16, 8, SHARE), vmem(F32, 16, 8, 128), vmem(F32, 8, SHARE), vmem(F32, 8, 128)]
        + [vmem(F32, 8, CHANNELS)]
        + [vmem(F32, 2, ROWS, SPAN)]
        + [
            pltpu.SemaphoreType.DMA((2, 3, CHUNKS)),
            pltpu.SemaphoreType.DMA((14,)),
            pltpu.SemaphoreType.DMA((2, 2, 2, 16)),
        ],
        compiler_params=params(collective_id=1, has_side_effects=True),
        name="blocks",
    )(
        *[mixer_in] * 4, *[conv_weight] * 3, *[conv_bias] * 3, grad_out, step_raw, step_bias,
        decay_log, skip_gain,
    )


def call_edge(y, grad, dstep, after, total, conv_weight):
    far = pl.BlockSpec(memory_space=pl.ANY)
    heads = sds((1, HEADS), F32)
    return pl.pallas_call(
        edge_kernel,
        in_specs=[far, far] + [VMEM] * 4,
        out_specs=[far, far] + [VMEM] * 6,
        out_shape=[sds(y.shape, BF16), sds(grad.shape, BF16), sds(dstep.shape, BF16)]
        + [sds((CONV, CHANNELS), F32), sds((1, CHANNELS), F32)]
        + [heads] * 3,
        scratch_shapes=[
            pltpu.VMEM(y.shape, BF16),
            pltpu.VMEM(grad.shape, BF16),
            pltpu.SemaphoreType.DMA((2, 2, ROWS // EDGE)),
        ],
        compiler_params=params(),
        name="edge",
    )(y, grad, dstep, after, total, conv_weight)


def on_device(
    mixer_in, step_raw, step_bias, decay_log, skip_gain, conv_weight, conv_bias, grad_out
):
    y, grad, dstep, after, total = call_blocks(
        mixer_in, conv_weight, conv_bias[None], grad_out, step_raw, step_bias[None],
        decay_log[None], skip_gain[None],
    )
    y, grad, dstep, gw, gv, h0, h1, h2 = call_edge(y, grad, dstep, after, total, conv_weight)
    return (y, grad, dstep, gw, gv[0], h0[0], h1[0], h2[0])


def solution(mesh):
    rows = P(("dp", "ctx"), None)
    in_specs = (rows, rows, P(), P(), P(), P(), P(), rows)
    out_specs = (rows, rows, rows, P("dp", None), P("dp"), P("dp"), P("dp"), P("dp"))
    return jax.shard_map(
        on_device, mesh=mesh, in_specs=in_specs, out_specs=out_specs, check_vma=False
    )
```

```python
import functools
import math

import jax
import jax.numpy as jnp
from jax import lax
from jax.experimental import pallas as pl
from jax.experimental.pallas import tpu as pltpu
from jax.sharding import PartitionSpec as P

HEADS = 128
HEAD_DIM = 64
GROUPS = 8
STATE = 128
CONV = 4
ROWS = 256
HALF = ROWS // 2
INNER = HEADS * HEAD_DIM
SPAN = GROUPS * STATE
CHANNELS = INNER + 2 * SPAN
WIDTH = INNER // GROUPS
PAIRS = WIDTH // 128
BLOCKS = CHANNELS // WIDTH
CHUNKS = 8
PIECE = STATE * GROUPS // CHUNKS
LAG = 2
LEAD = 2
LOG2E = math.log2(math.e)
F32 = jnp.float32
BF16 = jnp.bfloat16
MESH = pl.DeviceIdType.MESH
VMEM_LIMIT = 62 * 1024 * 1024


def dot(left, right):
    return jnp.dot(left, right, preferred_element_type=F32)


def dot_nt(left, right):
    return lax.dot_general(left, right, (((1,), (1,)), ((), ())), preferred_element_type=F32)


def dot_tn(left, right):
    return lax.dot_general(left, right, (((0,), (0,)), ((), ())), preferred_element_type=F32)


def pair_columns(values, first):
    return tuple(
        jnp.broadcast_to(values[:, first + i : first + i + 1], (ROWS, 128)) for i in range(2)
    )


def pair_lanes(values, first, low):
    return jnp.where(low, *pair_columns(values, first))


def head_picks():
    lanes = lax.broadcasted_iota(jnp.int32, (WIDTH, HEADS), 0)
    heads = lax.broadcasted_iota(jnp.int32, (WIDTH, HEADS), 1)
    return (heads == lanes // HEAD_DIM).astype(F32).astype(BF16)


def low_half():
    return lax.broadcasted_iota(jnp.int32, (ROWS, 128), 1) < HEAD_DIM


SECOND = GROUPS
THIRD = 2 * GROUPS
STEPS = THIRD + BLOCKS
SHARE = INNER // 16
EDGE = 64
EARLY = (GROUPS - 2) * WIDTH // SHARE


def lanes_at(j):
    if isinstance(j, int):
        return slice(j * 128, (j + 1) * 128)
    return pl.ds(pl.multiple_of(j * 128, 128), 128)


def stack(*pieces):
    return jnp.concatenate(pieces, 0)


def beside(*pieces):
    return jnp.concatenate(pieces, 1)


def scores_of(group, j, dy_ref, scaled_ref, ldg_ref, ldt_ref, contact, dcontact, in_ref, ds_ref):
    lanes = lanes_at(j)
    first = group * (2 * PAIRS) + 2 * j
    low = low_half()
    rows = lax.broadcasted_iota(jnp.int32, (HALF, HALF), 0)
    causal = rows >= lax.broadcasted_iota(jnp.int32, (HALF, HALF), 1)
    dy = dy_ref[:, lanes]
    scaled = scaled_ref[:, lanes]
    zero = jnp.zeros_like(dy)
    dys = (jnp.where(low, dy, zero), jnp.where(low, zero, dy))
    xs = (jnp.where(low, scaled, zero), jnp.where(low, zero, scaled))
    top = dot_nt(stack(dys[0][:HALF], dys[1][:HALF]), scaled[:HALF])
    bottom = dot_nt(stack(dys[0][HALF:], dys[1][HALF:]), scaled)
    lds = pair_columns(ldg_ref[...], 2 * j)
    tiles = []
    for half in range(2):
        row = ldt_ref[pl.ds(first + half, 1), :]
        here = slice(HALF * half, HALF * half + HALF)
        for tile, mine, cols, grad in (
            (0, slice(0, HALF), slice(0, HALF), top[here]),
            (1, slice(HALF, ROWS), slice(0, HALF), bottom[here, :HALF]),
            (2, slice(HALF, ROWS), slice(HALF, ROWS), bottom[here, HALF:]),
        ):
            gap = lds[half][mine] - row[:, cols]
            if tile != 1:
                gap = jnp.where(causal, gap, -1e30)
            decay = jnp.exp2(gap)
            tiles.append((contact[tile] * decay).astype(BF16))
            dcontact[tile] += grad * decay
    in_ref[:HALF, lanes] = dot(beside(tiles[0], tiles[3]), stack(xs[0][:HALF], xs[1][:HALF]))
    in_ref[HALF:, lanes] = dot(beside(tiles[1], tiles[2], tiles[4], tiles[5]), stack(*xs))
    ds_ref[:HALF, lanes] = dot_tn(stack(tiles[0], tiles[1], tiles[3], tiles[4]), stack(*dys))
    ds_ref[HALF:, lanes] = dot_tn(stack(tiles[2], tiles[5]), stack(dys[0][HALF:], dys[1][HALF:]))


def start_tiles(b, c, contact, dcontact):
    contact[0] = dot_nt(c[:HALF], b[:HALF])
    both = dot_nt(c[HALF:], b)
    contact[1] = both[:, :HALF]
    contact[2] = both[:, HALF:]
    dcontact[...] = jnp.zeros_like(dcontact)


def end_tiles(b, c, dcontact, dbw_ref, dcw_ref):
    tiles = dcontact[...].astype(BF16)
    dbw_ref[:HALF] = dot_tn(stack(tiles[0], tiles[1]), c)
    dbw_ref[HALF:] = dot_tn(tiles[2], c[HALF:])
    dcw_ref[:HALF] = dot(tiles[0], b[:HALF])
    dcw_ref[HALF:] = dot(beside(tiles[1], tiles[2]), b)


def block_kernel(
    raw_ref, raw_b_ref, raw_c_ref, mixer_ref, weight_ref, weight_b_ref, weight_c_ref,
    bias_ref, bias_b_ref, bias_c_ref, dy_ref, step_ref, step_bias_ref, decay_ref, skip_ref,
    y_ref, grad_ref, dstep_ref, after_ref, total_ref,
    acts, slopes, xs, inners, dscales, fg, given, above, below, came,
    halo, fade, fades, skips, dts, dtg, ldg, ldt, shifted, contact, dcontact,
    ends, begins, nets, grows, heads, net_sum, grow_sum, head_sum, picks,
    wsum, first, after, parts_x, parts_bc, mine_x, mine_bc, total, dacts,
    sems, edge_sems, total_sems,
):
    at = pl.program_id(0)
    index = lax.axis_index("ctx")
    count = lax.axis_size("ctx")
    core, chip = lax.rem(index, 2), index // 2
    own = 1 - core
    partner = index + 1 - 2 * core
    ahead = lax.rem(index + 2, count)
    behind = lax.rem(index + count - 2, count)
    down = jnp.where(core == 1, ahead, behind)
    place = jnp.where(core == 1, chip, count // 2 - 1 - chip)
    has_up = place > 0
    has_down = place < count // 2 - 1
    following = lax.rem(index + 1, count)
    previous = lax.rem(index + count - 1, count)
    block = jnp.where(at < SECOND, at, at - THIRD)

    def remote(src, dst, send, recv, to):
        return pltpu.make_async_remote_copy(
            src_ref=src, dst_ref=dst, send_sem=send, recv_sem=recv,
            device_id={"ctx": to}, device_id_type=MESH,
        )

    def copy(kind, q, src, dst, to):
        return remote(src, dst, sems.at[0, kind, q], sems.at[1, kind, q], to)

    def give(q):
        return copy(0, q, fg.at[core, q], given.at[q], partner)

    def pass_on(q):
        return copy(1, q, below.at[q], above.at[q], down)

    def share(q):
        return copy(2, q, above.at[q], came.at[q], partner)

    tail = mixer_ref.at[pl.ds(ROWS - 16, 16), :]
    x_cols, bc_cols = pl.ds(0, INNER), pl.ds(INNER, 2 * SPAN)
    near_cols, far_cols = pl.ds(0, WIDTH), pl.ds(WIDTH, INNER - WIDTH)

    def halo_copy(kind, cols):
        return remote(
            tail.at[:, cols], halo.at[:, cols],
            edge_sems.at[8 + 2 * kind], edge_sems.at[9 + 2 * kind], following,
        )


    def first_copy(kind, cols):
        return remote(
            first.at[:, cols], after.at[:, cols],
            edge_sems.at[4 + 2 * kind], edge_sems.at[5 + 2 * kind], previous,
        )

    def share_cols(kind, i):
        if kind == 0:
            return pl.ds(pl.multiple_of(i * SHARE, 128), SHARE)
        return pl.ds(pl.multiple_of(INNER + i * 128, 128), 128)

    parts, mine = (parts_x, parts_bc), (mine_x, mine_bc)

    def part_copy(kind, sender, to):
        return remote(
            wsum.at[:, share_cols(kind, to)], parts[kind].at[sender],
            total_sems.at[kind, 0, 0, to], total_sems.at[kind, 0, 1, sender], to,
        )

    def total_copy(kind, sender, to):
        return remote(
            mine[kind], total.at[:, share_cols(kind, sender)],
            total_sems.at[kind, 1, 0, to], total_sems.at[kind, 1, 1, sender], to,
        )

    def others(body):
        def step(i, carry):
            body(lax.rem(index + i, count))
            return carry

        lax.fori_loop(1, count, step, 0)

    fade_copy = remote(fade, fades, edge_sems.at[2], edge_sems.at[3], partner)

    @pl.when(at == 0)
    def _():
        barrier = pltpu.get_barrier_semaphore()
        others(
            lambda other: pl.semaphore_signal(
                barrier, inc=1, device_id={"ctx": other}, device_id_type=MESH
            )
        )
        pl.semaphore_wait(barrier, count - 1)
        halo_copy(0, bc_cols).start()
        halo_copy(1, near_cols).start()
        halo_copy(2, far_cols).start()

        dt = jax.nn.softplus(step_ref[...].astype(F32) + step_bias_ref[...])
        ld = dt * (-jnp.exp(decay_ref[...]) * LOG2E)
        rows = lax.broadcasted_iota(jnp.int32, (ROWS, HEADS), 0)
        shift = 1
        while shift < ROWS:
            ld = ld + jnp.where(rows >= shift, pltpu.roll(ld, shift, 0), 0.0)
            shift *= 2
        dts[...] = dt
        ldt[...] = ld.T
        picks[...] = head_picks()
        wsum[...] = jnp.zeros_like(wsum)
        for group in range(GROUPS):
            shift = (HEADS - group * 2 * PAIRS) % HEADS
            dtg[group] = pltpu.roll(dt, shift, 1) if shift else dt
            ldg[group] = pltpu.roll(ld, shift, 1) if shift else ld
        low = lax.broadcasted_iota(jnp.int32, (1, 128), 1) < HEAD_DIM
        for row, out in ((jnp.exp2(ld[ROWS - 1 : ROWS]), fade), (skip_ref[...], skips)):
            for group in range(GROUPS):
                for j in range(PAIRS):
                    at_head = group * 2 * PAIRS + 2 * j
                    pair = [
                        jnp.broadcast_to(row[:, at_head + i : at_head + i + 1], (1, 128))
                        for i in range(2)
                    ]
                    out[group : group + 1, lanes_at(j)] = jnp.where(low, *pair)
        fade_copy.start()

        @pl.when(jnp.logical_not(has_up))
        def _():
            above[...] = jnp.zeros_like(above)

        halo_copy(0, bc_cols).wait()
        halo_copy(1, near_cols).wait()

        @pl.when(index == 0)
        def _():
            halo[:, INNER:] = jnp.zeros((16, 2 * SPAN), BF16)
            halo[:, :WIDTH] = jnp.zeros((16, WIDTH), BF16)

    @pl.when(at == 1)
    def _():
        halo_copy(2, far_cols).wait()

        @pl.when(index == 0)
        def _():
            halo[:, WIDTH:INNER] = jnp.zeros((16, INNER - WIDTH), BF16)

        fade_copy.wait()

    def serve(q):
        block = q // (CHUNKS // GROUPS)
        mine = fade[pl.ds(block, 1), :]
        theirs = fades[pl.ds(block, 1), :]
        give(q).wait_recv()
        got = given[q].astype(F32)

        @pl.when(has_up)
        def _():
            pass_on(q).wait_recv()

        here = got + theirs * above[q].astype(F32)

        @pl.when(has_down)
        def _():
            below[q] = (fg[own, q].astype(F32) + mine * here).astype(BF16)
            pass_on(q).start()

        share(q).start()
        fg[own, q] = here.astype(BF16)

    def serve_at(slot):
        q = slot - LEAD - LAG * place
        pl.when(jnp.logical_and(q >= 0, q < CHUNKS))(functools.partial(serve, q))

    def block_lanes(j):
        return pl.ds(pl.multiple_of(block * WIDTH + j * 128, 128), 128)

    def conv(raw_of, weight, bias, lanes, kind, here, halo_lanes, slot):
        shifted[slot, 0:8, :] = halo[8:16, halo_lanes].astype(F32)
        raw = raw_of[:, lanes].astype(F32)
        shifted[slot, 8 : ROWS + 8, :] = raw
        pre = bias[:, lanes] + weight[CONV - 1 : CONV, lanes] * raw
        for k in range(CONV - 1):
            pre = pre + weight[k : k + 1, lanes] * shifted[slot, 5 + k : ROWS + 5 + k, :]
        gate = 1.0 / (1.0 + jnp.exp(-pre))
        act = pre * gate
        slopes[kind, :, here] = (gate + act * (1.0 - gate)).astype(BF16)
        rounded = act.astype(BF16)
        acts[kind, :, here] = rounded
        return rounded

    pl.when(at < THIRD + GROUPS)(lambda: serve_at(at))

    @pl.when(at < SECOND)
    def _():
        group = at
        per = CHUNKS // GROUPS
        where = lanes_at(group)
        turned = []
        for kind, raw_of, weight, bias in (
            (0, raw_b_ref, weight_b_ref, bias_b_ref),
            (1, raw_c_ref, weight_c_ref, bias_c_ref),
        ):
            base = INNER + kind * SPAN + group * STATE
            halo_lanes = pl.ds(pl.multiple_of(base, STATE), STATE)
            act = conv(raw_of, weight, bias, slice(0, STATE), GROUPS + kind, where, halo_lanes, kind)
            turned.append(act.T)
        low = low_half()
        for j in range(PAIRS):
            lanes = lanes_at(j)
            act = conv(
                raw_ref, weight_ref, bias_ref, lanes, group, lanes, block_lanes(j), j % 2
            )
            ld = pair_lanes(ldg[group], 2 * j, low)
            dt = pair_lanes(dtg[group], 2 * j, low)
            last = ld[ROWS - 1 : ROWS]
            scaled = (act.astype(F32) * dt).astype(BF16)
            xs[group, :, lanes] = scaled
            ends = (scaled.astype(F32) * jnp.exp2(last - ld)).astype(BF16)
            begins = (dy_ref[:, lanes].astype(F32) * jnp.exp2(ld)).astype(BF16)
            if j % 2 == 0:
                held = (ends, begins)
                continue
            lanes = slice((j - 1) * 128, (j + 1) * 128)
            for kind, piece in ((0, ends), (1, begins)):
                state = dot(turned[kind], beside(held[kind], piece)).astype(BF16)
                fg[kind, pl.ds(group * per, per), :, lanes] = state.reshape(per, PIECE, 256)

        def start_give(r, carry):
            give(group * per + r).start()
            return carry

        lax.fori_loop(0, per, start_give, 0)

    @pl.when(jnp.logical_and(at >= SECOND, at < THIRD))
    def _():
        group = at - SECOND
        where = lanes_at(group)
        b = acts[GROUPS, :, where]
        c = acts[GROUPS + 1, :, where]
        start_tiles(b, c, contact, dcontact)
        for j in range(PAIRS):
            scores_of(
                group, j, dy_ref, xs.at[group], ldg.at[group], ldt, contact, dcontact,
                inners.at[group], dscales.at[group],
            )
        end_tiles(b, c, dcontact, dacts.at[0, :, where], dacts.at[1, :, where])

    def conv_back(j, slot, dpre):
        lanes = lanes_at(j)
        here = block_lanes(j)
        first[:, here] = dpre[:16].astype(BF16)
        shifted[slot, 8 : ROWS + 8, :] = dpre
        raw = raw_ref[:, lanes].astype(F32)
        before = halo[8:16, here].astype(F32)
        grad = weight_ref[CONV - 1 : CONV, lanes] * dpre
        sums = []
        for k in range(CONV):
            moved = dpre
            if k < CONV - 1:
                moved = shifted[slot, 11 - k : ROWS + 11 - k, :]
                grad = grad + weight_ref[k : k + 1, lanes] * moved
            total = jnp.sum(raw * moved, 0, keepdims=True)
            if k < CONV - 1:
                edge = before * shifted[slot, 3 - k : 11 - k, :]
                total = total + jnp.sum(edge, 0, keepdims=True)
            sums.append(total)
        sums.append(jnp.sum(dpre, 0, keepdims=True))
        sums.append(jnp.zeros((3, 128), F32))
        grad_ref[:, lanes] = grad.astype(BF16)
        wsum[:, here] = jnp.concatenate(sums, 0)

    @pl.when(at == SECOND)
    def _():
        shifted[:, 0:8, :] = jnp.zeros((2, 8, 128), F32)
        shifted[:, ROWS + 8 : ROWS + 16, :] = jnp.zeros((2, 8, 128), F32)

    def add_up(kind):
        held = mine[kind]
        held[...] = wsum[:, share_cols(kind, index)]

        def add(sender):
            part_copy(kind, sender, index).wait_recv()
            held[...] += parts[kind][sender]

        others(add)
        others(lambda other: total_copy(kind, index, other).start())
        total[:, share_cols(kind, index)] = held[...]

    @pl.when(jnp.logical_and(at == THIRD + GROUPS - 1, index < EARLY))
    def _():
        add_up(0)

    @pl.when(jnp.logical_and(at >= THIRD, at < THIRD + GROUPS))
    def _():
        group = at - THIRD
        per = CHUNKS // GROUPS
        for r in range(per):
            q = group * per + r
            share(q).wait_recv()
            give(q).wait_send()
            fg[core, q] = came[q]
        where = lanes_at(group)
        b = acts[GROUPS, :, where]
        c = acts[GROUPS + 1, :, where]
        fade_row = fade[pl.ds(group, 1), :]
        skip_row = skips[pl.ds(group, 1), :]
        low = low_half()
        for j in range(PAIRS):
            lanes = lanes_at(j)
            ld = pair_lanes(ldg[group], 2 * j, low)
            dt = pair_lanes(dtg[group], 2 * j, low)
            act = acts[group, :, lanes].astype(F32)
            dy = dy_ref[:, lanes].astype(F32)
            scaled = xs[group, :, lanes].astype(F32)
            state = fg[0, pl.ds(group * per, per), :, lanes].reshape(STATE, 128)
            dstate = fg[1, pl.ds(group * per, per), :, lanes].reshape(STATE, 128)
            to_end = jnp.exp2(ld[ROWS - 1 : ROWS] - ld)
            from_start = jnp.exp2(ld)
            ends[:, lanes] = (scaled * to_end).astype(BF16)
            begins[:, lanes] = (dy * from_start).astype(BF16)
            inner = inners[group, :, lanes] + dot(c, state) * from_start
            dload = dot(b, dstate) * to_end
            dscaled = dscales[group, :, lanes] + dload
            skip = skip_row[:, lanes]
            y_ref[:, lanes] = (inner + skip * act).astype(BF16)
            grow = scaled * dscaled
            net = dy * inner - grow
            coarse = net.astype(BF16)
            nets[0, :, lanes] = coarse
            nets[1, :, lanes] = (net - coarse.astype(F32)).astype(BF16)
            grows[:, lanes] = grow.astype(BF16)
            ends_sum = jnp.sum(scaled * dload, 0, keepdims=True)
            ends_sum = ends_sum + fade_row[:, lanes] * jnp.sum(
                state.astype(F32) * dstate.astype(F32), 0, keepdims=True
            )
            skip_sum = jnp.sum(dy * act, 0, keepdims=True)
            heads[0:1, lanes] = ends_sum
            heads[1:2, lanes] = skip_sum
            conv_back(j, j % 2, (dt * dscaled + skip * dy) * slopes[block, :, lanes].astype(F32))

        net_sum[group] = dot(nets[0], picks[...]) + dot(nets[1], picks[...])
        grow_sum[group] = dot(grows[...], picks[...])
        rest = heads[...]
        total = jnp.zeros((8, HEADS), F32)
        for _ in range(3):
            piece = rest.astype(BF16)
            total = total + dot(piece, picks[...])
            rest = rest - piece.astype(F32)
        head_sum[group] = total
        state = fg[0, pl.ds(group * per, per)].reshape(STATE, WIDTH)
        dstate = fg[1, pl.ds(group * per, per)].reshape(STATE, WIDTH)
        dacts[0, :, where] += dot_nt(ends[...], dstate)
        dacts[1, :, where] += dot_nt(begins[...], state)

    @pl.when(at >= THIRD + GROUPS)
    def _():
        for j in range(PAIRS):
            lanes = lanes_at(j)
            conv_back(j, j % 2, dacts[at - THIRD - GROUPS, :, lanes] * slopes[block, :, lanes].astype(F32))

    @pl.when(at == THIRD + GROUPS)
    def _():
        lanes = lax.broadcasted_iota(jnp.int32, (ROWS, HEADS), 1)

        def of_heads(slabs):
            total = slabs[0]
            for group in range(1, GROUPS):
                moved = pltpu.roll(slabs[group], group * 2 * PAIRS, 1)
                here = lanes[: moved.shape[0]] >= group * 2 * PAIRS
                total = jnp.where(here, moved, total)
            return total

        dlog = of_heads(net_sum)
        extra = of_heads(head_sum)
        rows = lax.broadcasted_iota(jnp.int32, (ROWS, HEADS), 0)
        shift = 1
        while shift < ROWS:
            moved = pltpu.roll(dlog, ROWS - shift, 0)
            dlog = dlog + jnp.where(rows < ROWS - shift, moved, 0.0)
            shift *= 2
        dlog = dlog + extra[0:1]
        rates = -jnp.exp(decay_ref[...])
        dt = dts[...]
        gate = jax.nn.sigmoid(step_ref[...].astype(F32) + step_bias_ref[...])
        dstep = (of_heads(grow_sum) / dt + rates * dlog) * gate
        dstep_ref[...] = dstep.astype(BF16)
        wsum[5:6, INNER : INNER + HEADS] = jnp.sum(dstep, 0, keepdims=True)
        wsum[5:6, INNER + HEADS : INNER + 2 * HEADS] = rates * jnp.sum(dlog * dt, 0, keepdims=True)
        wsum[5:6, INNER + 2 * HEADS : INNER + 3 * HEADS] = extra[1:2]

    @pl.when(at >= THIRD)
    def _():
        def start_part(kind, i, carry):
            pl.when(i != index)(lambda: part_copy(kind, index, i).start())
            return carry

        @pl.when(at < THIRD + GROUPS)
        def _():
            k = (at - THIRD) * (WIDTH // SHARE)
            lax.fori_loop(k, k + WIDTH // SHARE, functools.partial(start_part, 0), 0)

        @pl.when(at >= THIRD + GROUPS)
        def _():
            k = (at - THIRD - GROUPS) * GROUPS
            lax.fori_loop(k, k + GROUPS, functools.partial(start_part, 1), 0)

    pl.when(at == THIRD + GROUPS - 1)(lambda: first_copy(0, x_cols).start())

    @pl.when(at == STEPS - 1)
    def _():
        first_copy(1, bc_cols).start()
        pl.when(index >= EARLY)(lambda: add_up(0))
        add_up(1)

        def finish(q, carry):
            @pl.when(has_down)
            def _():
                pass_on(q).wait_send()

            share(q).wait_send()
            return carry

        lax.fori_loop(0, CHUNKS, finish, 0)
        first_copy(0, x_cols).wait()
        first_copy(1, bc_cols).wait()
        after_ref[...] = after[...]

        def end(other):
            for kind in range(2):
                part_copy(kind, index, other).wait_send()
                total_copy(kind, index, other).wait_send()
                total_copy(kind, other, index).wait_recv()

        others(end)
        total_ref[...] = total[...]


def edge_kernel(
    y_in, grad_in, dstep_in, after_ref, total_ref, weight_ref,
    y_out, grad_out, dstep_out, gw_ref, gv_ref, h0_ref, h1_ref, h2_ref,
    y_held, grad_held, sems,
):
    count = y_in.shape[0] // EDGE
    pairs = []
    for kind, (src, held, dst) in enumerate(((grad_in, grad_held, grad_out), (y_in, y_held, y_out))):
        for i in range(count):
            rows = pl.ds((count - 1 - i) * EDGE, EDGE)
            pairs.append(
                (
                    pltpu.make_async_copy(src.at[rows], held.at[rows], sems.at[0, kind, i]),
                    pltpu.make_async_copy(held.at[rows], dst.at[rows], sems.at[1, kind, i]),
                )
            )
    for fetch, _ in pairs:
        fetch.start()
    dstep_out[...] = dstep_in[...]
    gw_ref[...] = total_ref[0:CONV]
    gv_ref[...] = total_ref[CONV : CONV + 1]
    for place, ref in enumerate((h0_ref, h1_ref, h2_ref)):
        start = INNER + place * HEADS
        ref[...] = total_ref[5:6, start : start + HEADS]
    last = lax.axis_index("ctx") == lax.axis_size("ctx") - 1
    after = jnp.where(last, 0.0, after_ref[0:8].astype(F32))
    rows = lax.broadcasted_iota(jnp.int32, after.shape, 0)
    more = jnp.zeros_like(after)
    for k in range(CONV - 1):
        moved = pltpu.roll(after, 5 + k, 0)
        more = more + jnp.where(rows >= 5 + k, weight_ref[k : k + 1] * moved, 0.0)
    more = jnp.concatenate([jnp.zeros_like(more), more], 0)
    for i, (fetch, store) in enumerate(pairs):
        fetch.wait()
        if i == 0:
            tail = grad_held[ROWS - 16 :].astype(F32) + more
            grad_held[ROWS - 16 :] = tail.astype(BF16)
        store.start()
    for _, store in pairs:
        store.wait()


def params(**kw):
    return pltpu.CompilerParams(vmem_limit_bytes=VMEM_LIMIT, **kw)


sds = jax.ShapeDtypeStruct
VMEM = pl.BlockSpec(memory_space=pltpu.VMEM)


def whole(*shape):
    return pl.BlockSpec(shape, lambda g: (0,) * len(shape))


def columns_of(rows, pick, width=WIDTH):
    return pl.BlockSpec((rows, width), lambda g: (0, pick(g)))


def same(g):
    return g


def call_blocks(
    mixer_in, conv_weight, conv_bias, grad_out, step_raw, step_bias, decay_log, skip_gain
):
    def block(g):
        return jnp.where(g < SECOND, g, jnp.maximum(g - THIRD, 0))

    def group(g):
        early = jnp.where(g < SECOND, g, g - SECOND)
        return jnp.where(g < THIRD, early, jnp.minimum(g - THIRD, GROUPS - 1))

    def b_block(g):
        return INNER // STATE + jnp.minimum(g, GROUPS - 1)

    def c_block(g):
        return (INNER + SPAN) // STATE + jnp.minimum(g, GROUPS - 1)

    def three(rows):
        return [
            columns_of(rows, block),
            columns_of(rows, b_block, STATE),
            columns_of(rows, c_block, STATE),
        ]

    def y_block(g):
        return jnp.clip(g - THIRD, 0, GROUPS - 1)

    def grad_block(g):
        return jnp.maximum(g - THIRD, 0)

    def vmem(dtype, *shape):
        return pltpu.VMEM(shape, dtype)

    pieces = vmem(BF16, CHUNKS, PIECE, WIDTH)
    return pl.pallas_call(
        block_kernel,
        grid=(STEPS,),
        in_specs=three(ROWS)
        + [pl.BlockSpec(memory_space=pl.ANY)]
        + three(CONV)
        + three(1)
        + [columns_of(ROWS, group)]
        + [whole(ROWS, HEADS)]
        + [whole(1, HEADS)] * 3,
        out_specs=[columns_of(ROWS, y_block), columns_of(ROWS, grad_block)] + [VMEM] * 3,
        out_shape=[sds((ROWS, INNER), BF16), sds((ROWS, CHANNELS), BF16), sds((ROWS, HEADS), BF16)]
        + [sds((16, CHANNELS), BF16), sds((8, CHANNELS), F32)],
        scratch_shapes=[vmem(BF16, BLOCKS, ROWS, WIDTH)] * 2
        + [vmem(BF16, GROUPS, ROWS, WIDTH)]
        + [vmem(F32, GROUPS, ROWS, WIDTH)] * 2
        + [vmem(BF16, 2, CHUNKS, PIECE, WIDTH)]
        + [pieces] * 4
        + [vmem(BF16, 16, CHANNELS)]
        + [vmem(F32, GROUPS, WIDTH)] * 3
        + [vmem(F32, ROWS, HEADS), vmem(F32, GROUPS, ROWS, HEADS), vmem(F32, GROUPS, ROWS, HEADS)]
        + [vmem(F32, HEADS, ROWS), vmem(F32, 2, ROWS + 16, 128)]
        + [vmem(F32, 3, HALF, HALF)] * 2
        + [vmem(BF16, ROWS, WIDTH)] * 2
        + [vmem(BF16, 2, ROWS, WIDTH), vmem(BF16, ROWS, WIDTH), vmem(F32, 8, WIDTH)]
        + [vmem(F32, GROUPS, ROWS, HEADS)] * 2
        + [vmem(F32, GROUPS, 8, HEADS), vmem(BF16, WIDTH, HEADS)]
        + [vmem(F32, 8, CHANNELS), vmem(BF16, 16, CHANNELS), vmem(BF16, 16, CHANNELS)]
        + [vmem(F32, 16, 8, SHARE), vmem(F32, 16, 8, 128), vmem(F32, 8, SHARE), vmem(F32, 8, 128)]
        + [vmem(F32, 8, CHANNELS)]
        + [vmem(F32, 2, ROWS, SPAN)]
        + [
            pltpu.SemaphoreType.DMA((2, 3, CHUNKS)),
            pltpu.SemaphoreType.DMA((14,)),
            pltpu.SemaphoreType.DMA((2, 2, 2, 16)),
        ],
        compiler_params=params(collective_id=1, has_side_effects=True),
        name="blocks",
    )(
        *[mixer_in] * 4, *[conv_weight] * 3, *[conv_bias] * 3, grad_out, step_raw, step_bias,
        decay_log, skip_gain,
    )


def call_edge(y, grad, dstep, after, total, conv_weight):
    far = pl.BlockSpec(memory_space=pl.ANY)
    heads = sds((1, HEADS), F32)
    return pl.pallas_call(
        edge_kernel,
        in_specs=[far, far] + [VMEM] * 4,
        out_specs=[far, far] + [VMEM] * 6,
        out_shape=[sds(y.shape, BF16), sds(grad.shape, BF16), sds(dstep.shape, BF16)]
        + [sds((CONV, CHANNELS), F32), sds((1, CHANNELS), F32)]
        + [heads] * 3,
        scratch_shapes=[
            pltpu.VMEM(y.shape, BF16),
            pltpu.VMEM(grad.shape, BF16),
            pltpu.SemaphoreType.DMA((2, 2, ROWS // EDGE)),
        ],
        compiler_params=params(),
        name="edge",
    )(y, grad, dstep, after, total, conv_weight)


def on_device(
    mixer_in, step_raw, step_bias, decay_log, skip_gain, conv_weight, conv_bias, grad_out
):
    y, grad, dstep, after, total = call_blocks(
        mixer_in, conv_weight, conv_bias[None], grad_out, step_raw, step_bias[None],
        decay_log[None], skip_gain[None],
    )
    y, grad, dstep, gw, gv, h0, h1, h2 = call_edge(y, grad, dstep, after, total, conv_weight)
    return (y, grad, dstep, gw, gv[0], h0[0], h1[0], h2[0])


def solution(mesh):
    rows = P(("dp", "ctx"), None)
    in_specs = (rows, rows, P(), P(), P(), P(), P(), rows)
    out_specs = (rows, rows, rows, P("dp", None), P("dp"), P("dp"), P("dp"), P("dp"))
    return jax.shard_map(
        on_device, mesh=mesh, in_specs=in_specs, out_specs=out_specs, check_vma=False
    )
```
